32 devices in a mesh: clip: 2 (over x), frame: 8 (over z, y), band: 2 (over core).
Axes of the slice: x: 2, y: 2, z: 4, core: 2. Of those that a mesh axis runs over, the one named last changes fastest.
Arguments:
- pixels: bfloat16 [16, 16, 32, 256], P(('clip', 'frame'), 'band'), parts along dimension 0, may hold values from -40 to 40
- gru_state: bfloat16 [16, 16, 32, 128], P(('clip', 'frame'), 'band'), parts along dimension 0, may hold values from -1 to 1
- tokens: bfloat16 [16, 1024, 256], P(('clip', 'frame'), 'band'), parts along dimension 0, may hold values from -30 to 30
- visible: int32 [16, 1024], P(('clip', 'frame'), 'band'), parts along dimension 0, may hold values from 0 to 1, as said below
- query_frame: int32 [2048], P(('clip', 'band')), parts along dimension 0, may hold values from 0 to 7, as said below
- pixel_query: bfloat16 [256, 256], replicated, may hold values from -2 to 2
- pixel_key: bfloat16 [256, 256], replicated, may hold values from -2 to 2
- pixel_value: bfloat16 [256, 256], replicated, may hold values from -0.375 to 0.375
- pixel_out: bfloat16 [256, 128], replicated, may hold values from -1.5 to 1.5
- time_query: bfloat16 [256, 256], replicated, may hold values from -2 to 2
- time_key: bfloat16 [256, 256], replicated, may hold values from -2 to 2
- time_value: bfloat16 [256, 256], replicated, may hold values from -0.375 to 0.375
- time_out: bfloat16 [256, 256], replicated, may hold values from -0.75 to 0.75
- gru_gates: bfloat16 [3, 3, 256, 256], replicated, may hold values from -0.125 to 0.125
- gru_candidate: bfloat16 [3, 3, 256, 128], replicated, may hold values from -0.125 to 0.125
Outputs:
- refined_state: bfloat16 [16, 16, 32, 128], P(('clip', 'frame'), 'band'), parts along dimension 0
- track_out: bfloat16 [16, 1024, 256], P(('clip', 'frame'), 'band'), parts along dimension 0
The draws below stay inside these ranges and needn't reach their ends.
There are 2 independent parts, one for each index of `clip`. The reference program is written for one: setup_inputs(seed, part) draws one part's arguments, and reference() takes and returns one part's arrays. A program takes and returns all parts, laid end to end along the dimension named above; an argument that names none is the same for every part. Nothing has to cross between parts.
Inputs may be any that keep to these rules, and one draw needn't show every extreme that they name: Each track is visible in the frame named by its query frame index. `query_frame`: every frame is the query frame of exactly 128 tracks.
All inputs are finite; a program needn't handle non-finite values.
Results may differ from the reference program's by a relative error of at most 0.0095.
The reference program's roundings to bfloat16 on the way count: a program that leaves them out, or rounds other values in their place, can miss the bound.
Values may be sent and summed in bfloat16 or wider, within the bound.
No kernel may reach another device: no remote copies, remote signals or barrier semaphores. Data moves between devices by JAX's collectives and lax.ppermute only.
A program may use at most 64 MiB of HBM per device.

```python
import math
import jax
import jax.numpy as jnp
from jax import lax

CHANNELS = 256
HEADS = 8
HEAD_DIM = 32
GRU_WIDTH = 128
TRACKS = 1024
WIDTH = 32
ITERS = 2
FRAMES = 8
ROWS = 16


def draw_pixels(key, part):
    full_shape = (FRAMES, ROWS, WIDTH, CHANNELS)
    drawn = jnp.clip(jax.random.normal(jax.random.fold_in(key, 502), full_shape, jnp.float32), -4.0, 4.0)
    return drawn.astype(jnp.bfloat16)


def draw_tokens(key, part):
    full_shape = (FRAMES, TRACKS, CHANNELS)
    drawn = jnp.clip(jax.random.normal(jax.random.fold_in(key, 506), full_shape, jnp.float32), -4.0, 4.0)
    return drawn.astype(jnp.bfloat16)


def track_layout(key):
    shuffled = jax.random.permutation(jax.random.fold_in(key, 701), TRACKS)
    anchor_frames = (shuffled % FRAMES).astype(jnp.int32)
    coin_flips = jax.random.randint(jax.random.fold_in(key, 702), (FRAMES, TRACKS), 0, 5)
    frame_ids = jnp.arange(FRAMES, dtype=jnp.int32)[:, None]
    seen_mask = jnp.logical_or(coin_flips < 3, frame_ids == anchor_frames[None, :]).astype(jnp.int32)
    return (seen_mask, anchor_frames)


def draw_visible(key, part):
    return track_layout(key)[0]


def draw_query_frame(key, part):
    return track_layout(key)[1]


def weight_pair(key, salt):
    first = jnp.clip(jax.random.normal(jax.random.fold_in(key, salt), (CHANNELS, CHANNELS), jnp.float32), -4.0, 4.0)
    second = jnp.clip(jax.random.normal(jax.random.fold_in(key, salt + 1), (CHANNELS, CHANNELS), jnp.float32), -4.0, 4.0)
    return (first, second)


def query_weight(key, salt):
    first, second = weight_pair(key, salt)
    return (2.0 * first / math.sqrt(CHANNELS)).astype(jnp.bfloat16)


def key_weight(key, salt):
    first, second = weight_pair(key, salt)
    mixed = second / math.sqrt(CHANNELS)
    return mixed.astype(jnp.bfloat16)


def draw_pixel_query(key, part):
    return query_weight(key, 601)


def draw_pixel_key(key, part):
    return key_weight(key, 601)


def draw_time_query(key, part):
    return query_weight(key, 611)


def draw_time_key(key, part):
    return key_weight(key, 611)


def block_levels(key, extent, shards, least, high):
    def one(dim, shards_of):
        steps = jax.random.uniform(jax.random.fold_in(jax.random.fold_in(key, 6), dim), (shards_of,), jnp.float32, least / len(shards), high / len(shards))
        return jnp.repeat(jnp.exp(steps), extent[dim] // shards_of).reshape((-1,) + (1,) * (len(extent) - dim - 1))

    loudness = one(*shards[0])
    for cut in shards[1:]:
        loudness = loudness * one(*cut)
    return loudness


def normal_values(rng, extent, spread, reach, held_as=jnp.bfloat16):
    values = jax.random.normal(rng, extent, jnp.float32) * spread
    return jnp.minimum(jnp.maximum(values, -reach), reach).astype(held_as)


def setup_inputs(seed: int = 0, part: int = 0) -> dict:
    seeds = jax.random.split(jax.random.key(seed), 16)
    own_keys = jax.random.split(jax.random.fold_in(seeds[15], part), 16)
    pixels = draw_pixels(jax.random.fold_in(jax.random.fold_in(seeds[15], part), 71), part)
    gru_state = jnp.clip(jax.random.uniform(own_keys[1], (FRAMES, ROWS, WIDTH, GRU_WIDTH), jnp.float32, -1.0, 1.0) * block_levels(own_keys[1], (FRAMES, ROWS, WIDTH, GRU_WIDTH), ((0, 8), (1, 2)), -0.4, 0.0), -1.0, 1.0).astype(jnp.bfloat16)
    tokens = draw_tokens(jax.random.fold_in(jax.random.fold_in(seeds[15], part), 71), part)
    visible = draw_visible(jax.random.fold_in(jax.random.fold_in(seeds[15], part), 71), part)
    query_frame = draw_query_frame(jax.random.fold_in(jax.random.fold_in(seeds[15], part), 71), part)
    pixel_query = draw_pixel_query(jax.random.fold_in(seeds[15], 71), part)
    pixel_key = draw_pixel_key(jax.random.fold_in(seeds[15], 71), part)
    pixel_value = normal_values(seeds[7], (CHANNELS, CHANNELS), CHANNELS ** -0.5, 0.375)
    pixel_out = normal_values(seeds[8], (CHANNELS, GRU_WIDTH), (CHANNELS // 16) ** -0.5, 1.5)
    time_query = draw_time_query(jax.random.fold_in(seeds[15], 71), part)
    time_key = draw_time_key(jax.random.fold_in(seeds[15], 71), part)
    time_value = normal_values(seeds[11], (CHANNELS, CHANNELS), CHANNELS ** -0.5, 0.375)
    time_out = normal_values(seeds[12], (CHANNELS, CHANNELS), (CHANNELS // 4) ** -0.5, 0.75)
    gru_gates = normal_values(seeds[13], (3, 3, 2 * GRU_WIDTH, 2 * GRU_WIDTH), (18 * GRU_WIDTH) ** -0.5, 0.125)
    gru_candidate = normal_values(seeds[14], (3, 3, 2 * GRU_WIDTH, GRU_WIDTH), (18 * GRU_WIDTH) ** -0.5, 0.125)
    return dict(pixels=pixels, gru_state=gru_state, tokens=tokens, visible=visible, query_frame=query_frame, pixel_query=pixel_query, pixel_key=pixel_key, pixel_value=pixel_value, pixel_out=pixel_out, time_query=time_query, time_key=time_key, time_value=time_value, time_out=time_out, gru_gates=gru_gates, gru_candidate=gru_candidate)


def attend_heads(queries, key_rows, value_rows, key_mask):
    score_scale = HEAD_DIM ** -0.5
    head_outputs = []
    for head_index in range(HEADS):
        offset = head_index * HEAD_DIM
        scores = jnp.dot(queries[:, offset:offset + HEAD_DIM], key_rows[:, offset:offset + HEAD_DIM].T, preferred_element_type=jnp.float32) * score_scale
        scores = jnp.where(key_mask[None, :], scores, -jnp.inf)
        weights = jax.nn.softmax(scores, axis=-1).astype(jnp.bfloat16)
        head_outputs.append(jnp.dot(weights, value_rows[:, offset:offset + HEAD_DIM], preferred_element_type=jnp.float32))
    return jnp.concatenate(head_outputs, axis=-1).astype(jnp.bfloat16)


def conv_rows(padded, weight, rows, columns):
    widened = jnp.pad(padded, ((0, 0), (1, 1), (0, 0)))
    summed = jnp.zeros((rows * columns, weight.shape[3]), jnp.float32)
    for row_shift in range(3):
        for col_shift in range(3):
            window = widened[row_shift:row_shift + rows, col_shift:col_shift + columns]
            summed = summed + jnp.dot(window.reshape(rows * columns, -1), weight[row_shift, col_shift], preferred_element_type=jnp.float32)
    return summed


def reference(pixels, gru_state, tokens, visible, query_frame, pixel_query, pixel_key, pixel_value, pixel_out, time_query, time_key, time_value, time_out, gru_gates, gru_candidate):
    def frame_context(inputs):
        frame_pixels, frame_tokens, frame_seen = inputs
        queries = jnp.dot(frame_pixels.reshape(ROWS * WIDTH, CHANNELS), pixel_query, preferred_element_type=jnp.float32).astype(jnp.bfloat16)
        key_rows = jnp.dot(frame_tokens, pixel_key, preferred_element_type=jnp.float32).astype(jnp.bfloat16)
        value_rows = jnp.dot(frame_tokens, pixel_value, preferred_element_type=jnp.float32).astype(jnp.bfloat16)
        attended = attend_heads(queries, key_rows, value_rows, frame_seen > 0)
        return jnp.dot(attended, pixel_out, preferred_element_type=jnp.float32).astype(jnp.bfloat16).reshape(ROWS, WIDTH, GRU_WIDTH)

    context = lax.map(frame_context, (pixels, tokens, visible))

    def frame_refine(inputs):
        state_now, context_now = inputs
        for iteration in range(ITERS):
            combined = jnp.concatenate([state_now, context_now], axis=-1)
            padded = jnp.pad(combined, ((1, 1), (0, 0), (0, 0)))
            gate_terms = conv_rows(padded, gru_gates, ROWS, WIDTH)
            update = jax.nn.sigmoid(gate_terms[:, :GRU_WIDTH])
            reset_gate = jax.nn.sigmoid(gate_terms[:, GRU_WIDTH:])
            state_flat = state_now.reshape(ROWS * WIDTH, GRU_WIDTH).astype(jnp.float32)
            reset_state = (reset_gate * state_flat).astype(jnp.bfloat16).reshape(ROWS, WIDTH, GRU_WIDTH)
            mixed_in = jnp.concatenate([reset_state, context_now], axis=-1)
            padded_mix = jnp.pad(mixed_in, ((1, 1), (0, 0), (0, 0)))
            candidate = jnp.tanh(conv_rows(padded_mix, gru_candidate, ROWS, WIDTH))
            state_now = ((1.0 - update) * state_flat + update * candidate).astype(jnp.bfloat16).reshape(ROWS, WIDTH, GRU_WIDTH)
        return state_now

    refined_state = lax.map(frame_refine, (gru_state, context))

    flat_tokens = tokens.reshape(FRAMES * TRACKS, CHANNELS)
    time_queries = jnp.dot(flat_tokens, time_query, preferred_element_type=jnp.float32).astype(jnp.bfloat16).reshape(FRAMES, TRACKS, CHANNELS)
    time_keys = jnp.dot(flat_tokens, time_key, preferred_element_type=jnp.float32).astype(jnp.bfloat16).reshape(FRAMES, TRACKS, CHANNELS)
    time_values = jnp.dot(flat_tokens, time_value, preferred_element_type=jnp.float32).astype(jnp.bfloat16).reshape(FRAMES, TRACKS, CHANNELS)
    anchor = time_queries[query_frame, jnp.arange(TRACKS)]
    joint_queries = (time_queries.astype(jnp.float32) + anchor.astype(jnp.float32)[None]).astype(jnp.bfloat16)
    shaped = (FRAMES, TRACKS, HEADS, HEAD_DIM)
    scores = jnp.einsum("fthd,gthd->thfg", joint_queries.astype(jnp.float32).reshape(shaped), time_keys.astype(jnp.float32).reshape(shaped)) * (HEAD_DIM ** -0.5)
    key_mask = jnp.transpose(visible) > 0
    scores = jnp.where(key_mask[:, None, None, :], scores, -jnp.inf)
    weights = jax.nn.softmax(scores, axis=-1).astype(jnp.bfloat16)
    attended = jnp.einsum("thfg,gthd->fthd", weights.astype(jnp.float32), time_values.astype(jnp.float32).reshape(shaped))
    time_attended = attended.astype(jnp.bfloat16).reshape(FRAMES * TRACKS, CHANNELS)
    projected = jnp.dot(time_attended, time_out, preferred_element_type=jnp.float32).reshape(FRAMES, TRACKS, CHANNELS)
    track_out = (tokens.astype(jnp.float32) + projected).astype(jnp.bfloat16)
    return refined_state, track_out
```

```python
import jax
import jax.numpy as jnp
from jax import lax
from jax.experimental import pallas as pl
from jax.experimental.pallas import tpu as pltpu
from jax.sharding import PartitionSpec as P

HEADS = 8
ITERS = 2
LANES = 128
MASK_ROWS = 16
HIDDEN = -1e30

f32 = jnp.float32
bf16 = jnp.bfloat16
VMEM = pl.BlockSpec(memory_space=pltpu.VMEM)


def dot(a, b):
    return jnp.dot(a, b, preferred_element_type=f32)


def call(body, out, scratch, flops, *args, after=()):
    moved = sum(x.size * x.dtype.itemsize for x in args)
    return pl.pallas_call(
        lambda *refs: body(*refs[len(after) :]),
        out_shape=out,
        in_specs=[pl.BlockSpec(memory_space=pl.ANY)] * len(after) + [VMEM] * len(args),
        out_specs=jax.tree.map(lambda _: VMEM, out),
        scratch_shapes=scratch,
        compiler_params=pltpu.CompilerParams(vmem_limit_bytes=24 * 2**20),
        cost_estimate=pl.CostEstimate(flops=flops, bytes_accessed=moved, transcendentals=0),
    )(*after, *args)


def pack_body(tokens, visible, out):
    frames, rows, _ = out.shape
    share = tokens.shape[0] // frames
    flags = visible[...].astype(f32)
    for g in range(frames):
        part = tokens[g * share : (g + 1) * share, :]
        out[g, :share, :] = part[:, :LANES]
        out[g, share : 2 * share, :] = part[:, LANES:]
        first = g * share // LANES * LANES
        group = flags[:, first : first + LANES]
        out[g, 2 * share :, :] = jnp.broadcast_to(group, (MASK_ROWS, LANES)).astype(bf16)


def unpack(packed, share):
    frames = packed.shape[0]
    left = packed[:, :share, :].reshape(frames * share, LANES)
    right = packed[:, share : 2 * share, :].reshape(frames * share, LANES)
    return jnp.concatenate([left, right], axis=1)


def attend_body(
    tokens, visible, other, pixels, state, w_query, w_key, w_value, w_out, context, edge
):
    half, channels = tokens.shape
    frames = other.shape[0]
    share = half // frames
    head_dim = channels // HEADS
    rows = jnp.concatenate([tokens[...], unpack(other, share)], axis=0)
    key = dot(rows, w_key[...]).astype(bf16)
    value = dot(rows, w_value[...]).astype(bf16)
    query = dot(pixels[...], w_query[...]).astype(bf16)
    flags = [visible[...].astype(f32)]
    for first in range(0, half, LANES):
        flags.append(other[first // share, 2 * share :, :].astype(f32)[:1])
    bias = jnp.where(jnp.concatenate(flags, axis=1) > 0.5, 0.0, HIDDEN)
    head_of = lax.broadcasted_iota(jnp.int32, (1, channels), 1) // head_dim
    scale = head_dim**-0.5
    attended = jnp.zeros((pixels.shape[0], channels), f32)
    for head in range(HEADS):
        mine = head_of == head
        masked = jnp.where(mine, query, jnp.zeros_like(query))
        scores = lax.dot_general(
            masked, key, (((1,), (1,)), ((), ())), preferred_element_type=f32
        )
        scores = scores + bias
        top = jnp.max(scores, axis=1, keepdims=True)
        weights = jnp.exp((scores - top) * scale)
        total = jnp.sum(weights, axis=1, keepdims=True)
        summed = dot(weights.astype(bf16), value)
        attended = jnp.where(mine, summed / total, attended)
    context[...] = dot(attended.astype(bf16), w_out[...]).astype(bf16)
    count = edge.shape[0]
    start = pl.multiple_of((1 - lax.axis_index("band")) * (pixels.shape[0] - count), count)
    edge[:, :LANES] = state[pl.ds(start, count), :]
    edge[:, LANES:] = context[pl.ds(start, count), :]


def temporal_body(packed, query_frame, w_query, w_key, w_value, out, flag_cols, frame_cols):
    frames, share, channels = out.shape
    head_dim = channels // HEADS
    columns = -(-frames * HEADS // LANES) * LANES
    first = lax.axis_index("frame") * share
    group, start = first // LANES, pl.multiple_of(first % LANES, share)
    flags = packed[:, 2 * share :, :].reshape(frames * MASK_ROWS, LANES)
    flag_cols[...] = flags.astype(f32).T
    asked = query_frame[pl.ds(group, 1), :].astype(f32)
    frame_cols[...] = jnp.broadcast_to(asked, (LANES, LANES)).T
    flags = flag_cols[pl.ds(start, share), :]
    asked = frame_cols[pl.ds(start, share), :1]

    rows = unpack(packed, share)
    query = dot(rows, w_query[...]).astype(bf16).astype(f32).reshape(frames, share, channels)
    key = dot(rows, w_key[...]).astype(bf16).astype(f32).reshape(frames, share, channels)
    value = dot(rows, w_value[...]).astype(bf16).astype(f32).reshape(frames, share, channels)
    anchor = jnp.zeros((share, channels), f32)
    for f in range(frames):
        anchor = jnp.where(asked == f, query[f], anchor)

    head_of_row = lax.broadcasted_iota(jnp.int32, (channels, columns), 0) // head_dim
    column = lax.broadcasted_iota(jnp.int32, (channels, columns), 1)
    head_of_col = lax.broadcasted_iota(jnp.int32, (columns, channels), 1) // head_dim
    line = lax.broadcasted_iota(jnp.int32, (columns, channels), 0)
    scores = jnp.zeros((frames * share, columns), f32)
    for f in range(frames):
        joint = (query[f] + anchor).astype(bf16).astype(f32)
        product = (key * joint[None]).reshape(frames * share, channels)
        high = product.astype(bf16)
        low = (product - high.astype(f32)).astype(bf16)
        gather = jnp.where(column == head_of_row + f * HEADS, 1.0, 0.0).astype(bf16)
        scores = scores + dot(high, gather) + dot(low, gather)
    scores = scores.reshape(frames, share, columns) * head_dim**-0.5
    seen = [
        jnp.where(flags[:, g * MASK_ROWS : g * MASK_ROWS + 1] > 0.5, scores[g], HIDDEN)
        for g in range(frames)
    ]
    top = seen[0]
    for g in range(1, frames):
        top = jnp.maximum(top, seen[g])
    raised = [jnp.exp(s - top) for s in seen]
    total = raised[0]
    for g in range(1, frames):
        total = total + raised[g]
    weights = jnp.concatenate([r / total for r in raised], axis=0).astype(bf16)
    for f in range(frames):
        spread = jnp.where(line == head_of_col + f * HEADS, 1.0, 0.0).astype(bf16)
        wide = dot(weights, spread).reshape(frames, share, channels)
        out[f] = jnp.sum(wide * value, axis=0).astype(bf16)


def refine_body(state, context, halo, w_gates, w_cand, out, field, wide):
    taps, both, _ = w_gates.shape
    local, hidden = state.shape
    beyond = halo.shape[0]
    pixels = local + beyond
    width = (wide.shape[0] - pixels) // 2
    band = lax.axis_index("band")
    here = pl.multiple_of(band * beyond, beyond)
    there = pl.multiple_of((1 - band) * local, beyond)
    col = lax.broadcasted_iota(jnp.int32, (pixels, hidden), 0) % width
    wide[:width, :] = jnp.zeros((width, 3 * both), bf16)
    wide[width + pixels :, :] = jnp.zeros((width, 3 * both), bf16)

    def spread(values, lane):
        before = jnp.where(col == 0, 0.0, pltpu.roll(values, 1, 0))
        after = jnp.where(col == width - 1, 0.0, pltpu.roll(values, pixels - 1, 0))
        for c, shifted in enumerate((before, values, after)):
            first = c * both + lane
            wide[width : width + pixels, first : first + hidden] = shifted.astype(bf16)

    def conv(weight):
        rows = [wide[r * width : r * width + pixels, :] for r in range(3)]
        return dot(jnp.concatenate(rows, axis=1), weight[...].reshape(taps * both, -1))

    field[pl.ds(here, local), :] = context[...]
    field[pl.ds(there, beyond), :] = halo[:, hidden:]
    spread(field[...].astype(f32), hidden)
    field[pl.ds(here, local), :] = state[...]
    field[pl.ds(there, beyond), :] = halo[:, :hidden]
    now = field[...].astype(f32)
    for _ in range(ITERS):
        spread(now, 0)
        gates = conv(w_gates)
        update = jax.nn.sigmoid(gates[:, :hidden])
        reset = jax.nn.sigmoid(gates[:, hidden:])
        spread((reset * now).astype(bf16).astype(f32), 0)
        cand = jnp.tanh(conv(w_cand))
        now = ((1.0 - update) * now + update * cand).astype(bf16).astype(f32)
    field[...] = now.astype(bf16)
    out[...] = field[pl.ds(here, local), :]


def output_body(tokens, returned, w_out, out):
    out[...] = (tokens[...].astype(f32) + dot(returned[...], w_out[...])).astype(bf16)


def on_device(
    pixels,
    gru_state,
    tokens,
    visible,
    query_frame,
    pixel_query,
    pixel_key,
    pixel_value,
    pixel_out,
    time_query,
    time_key,
    time_value,
    time_out,
    gru_gates,
    gru_candidate,
):
    frames = lax.axis_size("frame")
    _, band_rows, width, channels = pixels.shape
    hidden = gru_state.shape[3]
    half = tokens.shape[1]
    share = half // frames
    local = band_rows * width
    beyond = 2 * ITERS * width
    assert lax.axis_size("band") == 2 and channels == 2 * LANES and hidden == LANES
    swap = [(0, 1), (1, 0)]
    local_tokens = tokens[0]
    flat_pixels = pixels.reshape(local, channels)
    flat_state = gru_state.reshape(local, hidden)

    packed = call(
        pack_body,
        jax.ShapeDtypeStruct((frames, 2 * share + MASK_ROWS, LANES), bf16),
        [],
        0,
        local_tokens,
        visible,
    )
    other = lax.ppermute(packed, "band", swap)
    arrived = lax.all_to_all(packed, "frame", split_axis=0, concat_axis=0, tiled=True)

    context, edge = call(
        attend_body,
        (
            jax.ShapeDtypeStruct((local, hidden), bf16),
            jax.ShapeDtypeStruct((beyond, 2 * hidden), bf16),
        ),
        [],
        4 * local * 2 * half * channels * HEADS,
        local_tokens,
        visible,
        other,
        flat_pixels,
        flat_state,
        pixel_query,
        pixel_key,
        pixel_value,
        pixel_out,
    )
    halo = lax.ppermute(edge, "band", swap)

    attended = call(
        temporal_body,
        jax.ShapeDtypeStruct((frames, share, channels), bf16),
        [
            pltpu.VMEM((LANES, frames * MASK_ROWS), f32),
            pltpu.VMEM((LANES, LANES), f32),
        ],
        6 * half * channels * channels * 4,
        arrived,
        query_frame.reshape(half // LANES, LANES),
        time_query,
        time_key,
        time_value,
        after=(edge,),
    )
    returned = lax.all_to_all(attended, "frame", split_axis=0, concat_axis=0, tiled=True)

    refined = call(
        refine_body,
        jax.ShapeDtypeStruct((local, hidden), bf16),
        [
            pltpu.VMEM((local + beyond, hidden), bf16),
            pltpu.VMEM((local + beyond + 2 * width, 6 * hidden), bf16),
        ],
        2 * (local + beyond) * 9 * 2 * hidden * 3 * hidden * ITERS,
        flat_state,
        context,
        halo,
        gru_gates.reshape(9, 2 * hidden, 2 * hidden),
        gru_candidate.reshape(9, 2 * hidden, hidden),
    )
    track_out = call(
        output_body,
        jax.ShapeDtypeStruct((half, channels), bf16),
        [],
        2 * half * channels * channels,
        local_tokens,
        returned.reshape(half, channels),
        time_out,
    )
    return refined.reshape(gru_state.shape), track_out[None]


def solution(mesh):
    placed = (
        P(("clip", "frame"), "band", None, None),
        P(("clip", "frame"), "band", None, None),
        P(("clip", "frame"), "band", None),
        P(("clip", "frame"), "band"),
        P(("clip", "band")),
        P(),
        P(),
        P(),
        P(),
        P(),
        P(),
        P(),
        P(),
        P(),
        P(),
    )
    return jax.shard_map(
        on_device,
        mesh=mesh,
        in_specs=placed,
        out_specs=(P(("clip", "frame"), "band", None, None), P(("clip", "frame"), "band", None)),
        check_vma=False,
    )
```

```python
import jax
import jax.numpy as jnp
from jax import lax
from jax.experimental import pallas as pl
from jax.experimental.pallas import tpu as pltpu
from jax.sharding import PartitionSpec as P

HEADS = 8
ITERS = 2
LANES = 128
MASK_ROWS = 16
HIDDEN = -1e30

f32 = jnp.float32
bf16 = jnp.bfloat16
VMEM = pl.BlockSpec(memory_space=pltpu.VMEM)
HBM = pl.BlockSpec(memory_space=pltpu.HBM)
LATER = pl.BlockSpec(memory_space=pl.ANY)


def dot(a, b):
    return jnp.dot(a, b, preferred_element_type=f32)


def call(body, out, near, far=(), scratch=(), flops=0, after=(), raw=(), grant=24 * 2**20, place=VMEM):
    moved = sum(x.size * x.dtype.itemsize for x in (*near, *far))

    def whole(*refs):
        refs = refs[len(after) :]
        if not far:
            return body(*refs)
        sources = refs[: len(far)]
        buffers, arrived = refs[-len(far) - 1 : -1], refs[-1]
        copies = [
            pltpu.make_async_copy(source, buffer, arrived.at[i])
            for i, (source, buffer) in enumerate(zip(sources, buffers))
        ]
        for copy in copies:
            copy.start()

        def fetch(copy, buffer):
            def wait():
                copy.wait()
                return buffer

            return wait

        fetched = [fetch(c, b) for c, b in zip(copies, buffers)]
        return body(*fetched, *refs[len(far) : -len(far) - 1])

    buffers = [pltpu.VMEM(x.shape, x.dtype) for x in far]
    if far:
        buffers.append(pltpu.SemaphoreType.DMA((len(far),)))
    return pl.pallas_call(
        whole,
        out_shape=out,
        in_specs=[LATER] * len(after) + [HBM] * len(raw + far) + [VMEM] * len(near),
        out_specs=jax.tree.map(lambda _: place, out),
        scratch_shapes=[*scratch, *buffers],
        compiler_params=pltpu.CompilerParams(vmem_limit_bytes=grant),
        cost_estimate=pl.CostEstimate(flops=flops, bytes_accessed=moved, transcendentals=0),
    )(*after, *raw, *far, *near)


def pack_body(tokens, visible, out, flags, packed, sems):
    frames, rows, _ = out.shape
    share = tokens.shape[1]
    chunks = 2
    step = frames // chunks
    first = pltpu.make_async_copy(visible, flags, sems.at[0])
    first.start()
    coming = []
    for i in range(chunks):
        some = pl.ds(i * step, step)
        coming.append(
            [
                pltpu.make_async_copy(
                    tokens.at[some, :, pl.ds(c * LANES, LANES)],
                    packed.at[some, pl.ds(c * share, share), :],
                    sems.at[1 + 2 * i + c],
                )
                for c in range(2)
            ]
        )
    for copies in coming:
        for copy in copies:
            copy.start()
    first.wait()
    for g in range(frames):
        group = flags[g * share // LANES, :].astype(f32)
        packed[g, 2 * share :, :] = jnp.broadcast_to(group[None], (MASK_ROWS, LANES)).astype(bf16)
    going = []
    for i, copies in enumerate(coming):
        for copy in copies:
            copy.wait()
        some = pl.ds(i * step, step)
        going.append(pltpu.make_async_copy(packed.at[some], out.at[some], sems.at[1 + 2 * chunks + i]))
        going[-1].start()
    for copy in going:
        copy.wait()


def attend_body(
    pixels, tokens, w_query, w_key, w_value, visible, w_out, state, other, flags, context, edge
):
    half, channels = other.shape
    head_dim = channels // HEADS
    query = dot(pixels()[...], w_query()[...]).astype(bf16)
    rows = jnp.concatenate([tokens()[...], other[...]], axis=0)
    key = dot(rows, w_key()[...]).astype(bf16)
    value = dot(rows, w_value()[...]).astype(bf16)
    bias = jnp.where(jnp.concatenate([visible()[...], flags[...]], axis=1) > 0, 0.0, HIDDEN)
    head_of = lax.broadcasted_iota(jnp.int32, (1, channels), 1) // head_dim
    scale = head_dim**-0.5
    attended = jnp.zeros(query.shape, f32)
    for head in range(HEADS):
        mine = head_of == head
        masked = jnp.where(mine, query, jnp.zeros_like(query))
        scores = lax.dot_general(
            masked, key, (((1,), (1,)), ((), ())), preferred_element_type=f32
        )
        scores = scores + bias
        top = jnp.max(scores, axis=1, keepdims=True)
        weights = jnp.exp((scores - top) * scale)
        total = jnp.sum(weights, axis=1, keepdims=True)
        summed = dot(weights.astype(bf16), value)
        attended = jnp.where(mine, summed / total, attended)
    context[...] = dot(attended.astype(bf16), w_out()[...]).astype(bf16)
    count = edge.shape[0]
    start = pl.multiple_of((1 - lax.axis_index("band")) * (query.shape[0] - count), count)
    edge[:, :LANES] = state()[pl.ds(start, count), :]
    edge[:, LANES:] = context[pl.ds(start, count), :]


def temporal_body(packed, query_frame, w_query, w_key, w_value, out, flag_cols, frame_cols, result, sems):
    frames, share, channels = out.shape
    head_dim = channels // HEADS
    columns = -(-frames * HEADS // LANES) * LANES
    me = lax.axis_index("frame")
    first = me * share
    group, start = first // LANES, pl.multiple_of(first % LANES, share)
    flags = packed[:, 2 * share :, :].reshape(frames * MASK_ROWS, LANES)
    flag_cols[...] = flags.astype(f32).T
    asked = query_frame[pl.ds(group, 1), :].astype(f32)
    frame_cols[...] = jnp.broadcast_to(asked, (LANES, LANES)).T
    flags = flag_cols[pl.ds(start, share), :]
    asked = frame_cols[pl.ds(start, share), :1]

    left = packed[:, :share, :].reshape(frames * share, LANES)
    right = packed[:, share : 2 * share, :].reshape(frames * share, LANES)
    rows = jnp.concatenate([left, right], axis=1)
    shape = (frames, share, channels)
    query = dot(rows, w_query[...]).astype(bf16).astype(f32).reshape(shape)
    key = dot(rows, w_key[...]).astype(bf16).astype(f32).reshape(shape)
    value = dot(rows, w_value[...]).astype(bf16).astype(f32).reshape(shape)
    anchor = jnp.zeros((share, channels), f32)
    for s in range(frames):
        anchor = jnp.where(asked == s, query[s], anchor)

    head_of_row = lax.broadcasted_iota(jnp.int32, (channels, columns), 0) // head_dim
    column = lax.broadcasted_iota(jnp.int32, (channels, columns), 1)
    head_of_col = lax.broadcasted_iota(jnp.int32, (columns, channels), 1) // head_dim
    line = lax.broadcasted_iota(jnp.int32, (columns, channels), 0)
    scores = jnp.zeros((frames * share, columns), f32)
    for s in range(frames):
        joint = (query[s] + anchor).astype(bf16).astype(f32)
        product = (key * joint[None]).reshape(frames * share, channels)
        high = product.astype(bf16)
        low = (product - high.astype(f32)).astype(bf16)
        gather = jnp.where(column == head_of_row + s * HEADS, 1.0, 0.0).astype(bf16)
        scores = scores + dot(high, gather) + dot(low, gather)
    scores = scores.reshape(frames, share, columns) * head_dim**-0.5
    seen = [
        jnp.where(flags[:, g * MASK_ROWS : g * MASK_ROWS + 1] > 0.5, scores[g], HIDDEN)
        for g in range(frames)
    ]
    top = seen[0]
    for g in range(1, frames):
        top = jnp.maximum(top, seen[g])
    raised = [jnp.exp(x - top) for x in seen]
    total = raised[0]
    for g in range(1, frames):
        total = total + raised[g]
    weights = jnp.concatenate([x / total for x in raised], axis=0).astype(bf16)
    copies = []
    for s in range(frames):
        spread = jnp.where(line == head_of_col + s * HEADS, 1.0, 0.0).astype(bf16)
        wide = dot(weights, spread).reshape(shape)
        result[s] = jnp.sum(wide * value, axis=0).astype(bf16)
        copies.append(pltpu.make_async_copy(result.at[s], out.at[s], sems.at[s]))
        copies[-1].start()
    for copy in copies:
        copy.wait()


def refine_body(state, context, halo, w_gates, w_cand, out, field, wide):
    taps, both, _ = w_gates.shape
    local, hidden = state.shape
    beyond = halo.shape[0]
    pixels = local + beyond
    width = (wide.shape[0] - pixels) // 2
    band = lax.axis_index("band")
    here = pl.multiple_of(band * beyond, beyond)
    there = pl.multiple_of((1 - band) * local, beyond)
    col = lax.broadcasted_iota(jnp.int32, (pixels, hidden), 0) % width
    wide[:width, :] = jnp.zeros((width, 3 * both), bf16)
    wide[width + pixels :, :] = jnp.zeros((width, 3 * both), bf16)

    def spread(values, lane):
        before = jnp.where(col == 0, 0.0, pltpu.roll(values, 1, 0))
        after = jnp.where(col == width - 1, 0.0, pltpu.roll(values, pixels - 1, 0))
        for c, shifted in enumerate((before, values, after)):
            first = c * both + lane
            wide[width : width + pixels, first : first + hidden] = shifted.astype(bf16)

    def conv(weight):
        rows = [wide[r * width : r * width + pixels, :] for r in range(3)]
        return dot(jnp.concatenate(rows, axis=1), weight[...].reshape(taps * both, -1))

    field[pl.ds(here, local), :] = context[...]
    field[pl.ds(there, beyond), :] = halo[:, hidden:]
    spread(field[...].astype(f32), hidden)
    field[pl.ds(here, local), :] = state[...]
    field[pl.ds(there, beyond), :] = halo[:, :hidden]
    now = field[...].astype(f32)
    for _ in range(ITERS):
        spread(now, 0)
        gates = conv(w_gates)
        update = jax.nn.sigmoid(gates[:, :hidden])
        reset = jax.nn.sigmoid(gates[:, hidden:])
        spread((reset * now).astype(bf16).astype(f32), 0)
        cand = jnp.tanh(conv(w_cand))
        now = ((1.0 - update) * now + update * cand).astype(bf16).astype(f32)
    field[...] = now.astype(bf16)
    out[...] = field[pl.ds(here, local), :]


def output_body(returned, tokens, w_out, out):
    out[...] = (tokens[...].astype(f32) + dot(returned[...], w_out[...])).astype(bf16)


def on_device(
    pixels,
    gru_state,
    tokens,
    visible,
    query_frame,
    pixel_query,
    pixel_key,
    pixel_value,
    pixel_out,
    time_query,
    time_key,
    time_value,
    time_out,
    gru_gates,
    gru_candidate,
):
    frames = lax.axis_size("frame")
    _, band_rows, width, channels = pixels.shape
    hidden = gru_state.shape[3]
    half = tokens.shape[1]
    share = half // frames
    local = band_rows * width
    beyond = 2 * ITERS * width
    assert LANES % share == 0
    assert lax.axis_size("band") == 2 and channels == 2 * LANES and hidden == LANES
    swap = [(0, 1), (1, 0)]
    local_tokens = tokens[0]
    flat_state = gru_state.reshape(local, hidden)
    groups = half // LANES

    other = lax.ppermute(local_tokens, "band", swap)
    flags = lax.ppermute(visible, "band", swap)
    packed = call(
        pack_body,
        jax.ShapeDtypeStruct((frames, 2 * share + MASK_ROWS, LANES), bf16),
        (),
        scratch=[
            pltpu.VMEM((groups, LANES), jnp.int32),
            pltpu.VMEM((frames, 2 * share + MASK_ROWS, LANES), bf16),
            pltpu.SemaphoreType.DMA((7,)),
        ],
        raw=(local_tokens.reshape(frames, share, channels), visible.reshape(groups, LANES)),
        flops=10**10,
        grant=60 * 2**20,
        place=HBM,
    )
    arrived = lax.all_to_all(packed, "frame", split_axis=0, concat_axis=0, tiled=True)

    context, edge = call(
        attend_body,
        (
            jax.ShapeDtypeStruct((local, hidden), bf16),
            jax.ShapeDtypeStruct((beyond, 2 * hidden), bf16),
        ),
        (other, flags),
        (
            pixels.reshape(local, channels),
            local_tokens,
            pixel_query,
            pixel_key,
            pixel_value,
            visible,
            pixel_out,
            flat_state,
        ),
        flops=4 * local * 2 * half * channels * HEADS,
    )
    halo = lax.ppermute(edge, "band", swap)

    attended = call(
        temporal_body,
        jax.ShapeDtypeStruct((frames, share, channels), bf16),
        (arrived, query_frame.reshape(groups, LANES), time_query, time_key, time_value),
        scratch=[
            pltpu.VMEM((LANES, frames * MASK_ROWS), f32),
            pltpu.VMEM((LANES, LANES), f32),
            pltpu.VMEM((frames, share, channels), bf16),
            pltpu.SemaphoreType.DMA((frames,)),
        ],
        place=HBM,
        flops=6 * half * channels * channels * 4,
        after=(edge,),
    )
    returned = lax.all_to_all(attended, "frame", split_axis=0, concat_axis=0, tiled=True)

    refined = call(
        refine_body,
        jax.ShapeDtypeStruct((local, hidden), bf16),
        (
            flat_state,
            context,
            halo,
            gru_gates.reshape(9, 2 * hidden, 2 * hidden),
            gru_candidate.reshape(9, 2 * hidden, hidden),
        ),
        scratch=[
            pltpu.VMEM((local + beyond, hidden), bf16),
            pltpu.VMEM((local + beyond + 2 * width, 6 * hidden), bf16),
        ],
        flops=2 * (local + beyond) * 9 * 2 * hidden * 3 * hidden * ITERS,
    )
    track_out = call(
        output_body,
        jax.ShapeDtypeStruct((half, channels), bf16),
        (returned.reshape(half, channels), local_tokens, time_out),
        flops=2 * half * channels * channels,
    )
    return refined.reshape(gru_state.shape), track_out[None]


def solution(mesh):
    placed = (
        P(("clip", "frame"), "band", None, None),
        P(("clip", "frame"), "band", None, None),
        P(("clip", "frame"), "band", None),
        P(("clip", "frame"), "band"),
        P(("clip", "band")),
        P(),
        P(),
        P(),
        P(),
        P(),
        P(),
        P(),
        P(),
        P(),
        P(),
    )
    return jax.shard_map(
        on_device,
        mesh=mesh,
        in_specs=placed,
        out_specs=(P(("clip", "frame"), "band", None, None), P(("clip", "frame"), "band", None)),
        check_vma=False,
    )
```

```python
import jax
import jax.numpy as jnp
from jax import lax
from jax.experimental import pallas as pl
from jax.experimental.pallas import tpu as pltpu
from jax.sharding import PartitionSpec as P

HEADS = 8
ITERS = 2
LANES = 128
MASK_ROWS = 16
HIDDEN = -1e30

f32 = jnp.float32
bf16 = jnp.bfloat16
VMEM = pl.BlockSpec(memory_space=pltpu.VMEM)
HBM = pl.BlockSpec(memory_space=pltpu.HBM)
LATER = pl.BlockSpec(memory_space=pl.ANY)


def dot(a, b):
    return jnp.dot(a, b, preferred_element_type=f32)


def call(body, out, near, far=(), scratch=(), flops=0, after=(), raw=(), grant=24 * 2**20, place=VMEM):
    moved = sum(x.size * x.dtype.itemsize for x in (*near, *far))

    def whole(*refs):
        refs = refs[len(after) :]
        if not far:
            return body(*refs)
        sources = refs[: len(far)]
        buffers, arrived = refs[-len(far) - 1 : -1], refs[-1]
        copies = [
            pltpu.make_async_copy(source, buffer, arrived.at[i])
            for i, (source, buffer) in enumerate(zip(sources, buffers))
        ]
        for copy in copies:
            copy.start()

        def fetch(copy, buffer):
            def wait():
                copy.wait()
                return buffer

            return wait

        fetched = [fetch(c, b) for c, b in zip(copies, buffers)]
        return body(*fetched, *refs[len(far) : -len(far) - 1])

    buffers = [pltpu.VMEM(x.shape, x.dtype) for x in far]
    if far:
        buffers.append(pltpu.SemaphoreType.DMA((len(far),)))
    return pl.pallas_call(
        whole,
        out_shape=out,
        in_specs=[LATER] * len(after) + [HBM] * len(raw + far) + [VMEM] * len(near),
        out_specs=jax.tree.map(lambda _: place, out),
        scratch_shapes=[*scratch, *buffers],
        compiler_params=pltpu.CompilerParams(vmem_limit_bytes=grant),
        cost_estimate=pl.CostEstimate(flops=flops, bytes_accessed=moved, transcendentals=0),
    )(*after, *raw, *far, *near)


def pack_body(tokens, visible, out, flags, packed, sems):
    frames, rows, _ = out.shape
    share = tokens.shape[1]
    chunks = 2
    step = frames // chunks
    first = pltpu.make_async_copy(visible, flags, sems.at[0])
    first.start()
    coming = []
    for i in range(chunks):
        some = pl.ds(i * step, step)
        coming.append(
            [
                pltpu.make_async_copy(
                    tokens.at[some, :, pl.ds(c * LANES, LANES)],
                    packed.at[some, pl.ds(c * share, share), :],
                    sems.at[1 + 2 * i + c],
                )
                for c in range(2)
            ]
        )
    for copies in coming:
        for copy in copies:
            copy.start()
    first.wait()
    for g in range(frames):
        group = flags[g * share // LANES, :].astype(f32)
        packed[g, 2 * share :, :] = jnp.broadcast_to(group[None], (MASK_ROWS, LANES)).astype(bf16)
    going = []
    for i, copies in enumerate(coming):
        for copy in copies:
            copy.wait()
        some = pl.ds(i * step, step)
        going.append(pltpu.make_async_copy(packed.at[some], out.at[some], sems.at[1 + 2 * chunks + i]))
        going[-1].start()
    for copy in going:
        copy.wait()


def attend_body(
    pixels,
    tokens,
    w_query,
    w_key,
    w_value,
    visible,
    w_out,
    state,
    w_time_query,
    w_time_key,
    w_time_value,
    other,
    flags,
    context,
    edge,
    w_time,
):
    half, channels = other.shape
    head_dim = channels // HEADS
    query = dot(pixels()[...], w_query()[...]).astype(bf16)
    rows = jnp.concatenate([tokens()[...], other[...]], axis=0)
    key = dot(rows, w_key()[...]).astype(bf16)
    value = dot(rows, w_value()[...]).astype(bf16)
    bias = jnp.where(jnp.concatenate([visible()[...], flags[...]], axis=1) > 0, 0.0, HIDDEN)
    head_of = lax.broadcasted_iota(jnp.int32, (1, channels), 1) // head_dim
    scale = head_dim**-0.5
    attended = jnp.zeros(query.shape, f32)
    for head in range(HEADS):
        mine = head_of == head
        masked = jnp.where(mine, query, jnp.zeros_like(query))
        scores = lax.dot_general(
            masked, key, (((1,), (1,)), ((), ())), preferred_element_type=f32
        )
        scores = scores + bias
        top = jnp.max(scores, axis=1, keepdims=True)
        weights = jnp.exp((scores - top) * scale)
        total = jnp.sum(weights, axis=1, keepdims=True)
        summed = dot(weights.astype(bf16), value)
        attended = jnp.where(mine, summed / total, attended)
    context[...] = dot(attended.astype(bf16), w_out()[...]).astype(bf16)
    count = edge.shape[0]
    start = pl.multiple_of((1 - lax.axis_index("band")) * (query.shape[0] - count), count)
    edge[:, :LANES] = state()[pl.ds(start, count), :]
    edge[:, LANES:] = context[pl.ds(start, count), :]
    for i, weight in enumerate((w_time_query, w_time_key, w_time_value)):
        w_time[i * channels : (i + 1) * channels, :] = weight()[...].astype(f32).T.astype(bf16)


def temporal_body(packed, query_frame, w_all, out, result, sems):
    frames, share, channels = out.shape
    head_dim = channels // HEADS
    tiles = frames * share // LANES
    beside = LANES // share
    me = lax.axis_index("frame")
    piece = lax.broadcasted_iota(jnp.int32, (1, LANES), 1) // share

    def fold(x, add=jnp.add):
        shift = share
        while shift < LANES:
            x = add(x, pltpu.roll(x, shift, 1))
            shift *= 2
        return x

    def everywhere(x, which):
        return fold(jnp.where(piece == which, x, 0.0))

    asked = query_frame[pl.ds(me * share // LANES, 1), :].astype(f32)
    asked = everywhere(asked, me % beside)
    flags = everywhere(packed[:, 2 * share, :].astype(f32), me % beside)
    seen = []
    for tile in range(tiles):
        row = jnp.zeros((1, LANES), f32)
        for o in range(beside):
            g = tile * beside + o
            row = jnp.where(piece == o, flags[g : g + 1, :], row)
        seen.append(row > 0.5)

    left = packed[:, :share, :].reshape(frames * share, LANES)
    right = packed[:, share : 2 * share, :].reshape(frames * share, LANES)
    rows = jnp.concatenate([left, right], axis=1)
    projected = lax.dot_general(
        w_all[...], rows, (((1,), (1,)), ((), ())), preferred_element_type=f32
    )
    projected = projected.astype(bf16).astype(f32)
    query, key, value = (
        [
            projected[i * channels : (i + 1) * channels, t * LANES : (t + 1) * LANES]
            for t in range(tiles)
        ]
        for i in range(3)
    )
    anchor = jnp.zeros((channels, LANES), f32)
    for tile in range(tiles):
        frame = (piece + tile * beside).astype(f32)
        anchor = anchor + jnp.where(asked == frame, query[tile], 0.0)
    anchor = fold(anchor)

    copies = []
    for tile in range(tiles):
        attended = jnp.zeros((channels, LANES), f32)
        for o in range(beside):
            joint = (everywhere(query[tile], o) + anchor).astype(bf16).astype(f32)
            scores = []
            for other in range(tiles):
                product = (key[other] * joint).reshape(HEADS, head_dim, LANES)
                score = jnp.sum(product, axis=1) * head_dim**-0.5
                scores.append(jnp.where(seen[other], score, HIDDEN))
            top = scores[0]
            for score in scores[1:]:
                top = jnp.maximum(top, score)
            top = fold(top, jnp.maximum)
            raised = [jnp.exp(score - top) for score in scores]
            total = fold(sum(raised[1:], raised[0]))
            summed = jnp.zeros((HEADS, head_dim, LANES), f32)
            for other in range(tiles):
                weight = (raised[other] / total).astype(bf16).astype(f32)
                here = value[other].reshape(HEADS, head_dim, LANES)
                summed = summed + here * weight[:, None, :]
            summed = fold(summed.reshape(channels, LANES))
            attended = jnp.where(piece == o, summed, attended)
        some = pl.ds(tile * beside, beside)
        result[some] = attended.T.astype(bf16).reshape(beside, share, channels)
        copies.append(pltpu.make_async_copy(result.at[some], out.at[some], sems.at[tile]))
        copies[-1].start()
    for copy in copies:
        copy.wait()


def refine_body(state, context, halo, w_gates, w_cand, out, field, wide):
    taps, both, _ = w_gates.shape
    local, hidden = state.shape
    beyond = halo.shape[0]
    pixels = local + beyond
    width = (wide.shape[0] - pixels) // 2
    band = lax.axis_index("band")
    here = pl.multiple_of(band * beyond, beyond)
    there = pl.multiple_of((1 - band) * local, beyond)
    col = lax.broadcasted_iota(jnp.int32, (pixels, hidden), 0) % width
    wide[:width, :] = jnp.zeros((width, 3 * both), bf16)
    wide[width + pixels :, :] = jnp.zeros((width, 3 * both), bf16)

    def spread(values, lane):
        before = jnp.where(col == 0, 0.0, pltpu.roll(values, 1, 0))
        after = jnp.where(col == width - 1, 0.0, pltpu.roll(values, pixels - 1, 0))
        for c, shifted in enumerate((before, values, after)):
            first = c * both + lane
            wide[width : width + pixels, first : first + hidden] = shifted.astype(bf16)

    def conv(weight):
        rows = [wide[r * width : r * width + pixels, :] for r in range(3)]
        return dot(jnp.concatenate(rows, axis=1), weight[...].reshape(taps * both, -1))

    field[pl.ds(here, local), :] = context[...]
    field[pl.ds(there, beyond), :] = halo[:, hidden:]
    spread(field[...].astype(f32), hidden)
    field[pl.ds(here, local), :] = state[...]
    field[pl.ds(there, beyond), :] = halo[:, :hidden]
    now = field[...].astype(f32)
    for _ in range(ITERS):
        spread(now, 0)
        gates = conv(w_gates)
        update = jax.nn.sigmoid(gates[:, :hidden])
        reset = jax.nn.sigmoid(gates[:, hidden:])
        spread((reset * now).astype(bf16).astype(f32), 0)
        cand = jnp.tanh(conv(w_cand))
        now = ((1.0 - update) * now + update * cand).astype(bf16).astype(f32)
    field[...] = now.astype(bf16)
    out[...] = field[pl.ds(here, local), :]


def output_body(returned, tokens, w_out, out):
    out[...] = (tokens[...].astype(f32) + dot(returned[...], w_out[...])).astype(bf16)


def on_device(
    pixels,
    gru_state,
    tokens,
    visible,
    query_frame,
    pixel_query,
    pixel_key,
    pixel_value,
    pixel_out,
    time_query,
    time_key,
    time_value,
    time_out,
    gru_gates,
    gru_candidate,
):
    frames = lax.axis_size("frame")
    _, band_rows, width, channels = pixels.shape
    hidden = gru_state.shape[3]
    half = tokens.shape[1]
    share = half // frames
    local = band_rows * width
    beyond = 2 * ITERS * width
    assert LANES % share == 0
    assert lax.axis_size("band") == 2 and channels == 2 * LANES and hidden == LANES
    swap = [(0, 1), (1, 0)]
    local_tokens = tokens[0]
    flat_state = gru_state.reshape(local, hidden)
    groups = half // LANES

    other = lax.ppermute(local_tokens, "band", swap)
    flags = lax.ppermute(visible, "band", swap)
    packed = call(
        pack_body,
        jax.ShapeDtypeStruct((frames, 2 * share + MASK_ROWS, LANES), bf16),
        (),
        scratch=[
            pltpu.VMEM((groups, LANES), jnp.int32),
            pltpu.VMEM((frames, 2 * share + MASK_ROWS, LANES), bf16),
            pltpu.SemaphoreType.DMA((7,)),
        ],
        raw=(local_tokens.reshape(frames, share, channels), visible.reshape(groups, LANES)),
        flops=10**10,
        grant=60 * 2**20,
        place=HBM,
    )
    arrived = lax.all_to_all(packed, "frame", split_axis=0, concat_axis=0, tiled=True)

    context, edge, w_time = call(
        attend_body,
        (
            jax.ShapeDtypeStruct((local, hidden), bf16),
            jax.ShapeDtypeStruct((beyond, 2 * hidden), bf16),
            jax.ShapeDtypeStruct((3 * channels, channels), bf16),
        ),
        (other, flags),
        (
            pixels.reshape(local, channels),
            local_tokens,
            pixel_query,
            pixel_key,
            pixel_value,
            visible,
            pixel_out,
            flat_state,
            time_query,
            time_key,
            time_value,
        ),
        flops=4 * local * 2 * half * channels * HEADS,
    )
    halo = lax.ppermute(edge, "band", swap)

    attended = call(
        temporal_body,
        jax.ShapeDtypeStruct((frames, share, channels), bf16),
        (arrived, query_frame.reshape(groups, LANES), w_time),
        scratch=[
            pltpu.VMEM((frames, share, channels), bf16),
            pltpu.SemaphoreType.DMA((frames,)),
        ],
        place=HBM,
        flops=6 * half * channels * channels * 4,
    )
    returned = lax.all_to_all(attended, "frame", split_axis=0, concat_axis=0, tiled=True)

    refined = call(
        refine_body,
        jax.ShapeDtypeStruct((local, hidden), bf16),
        (
            flat_state,
            context,
            halo,
            gru_gates.reshape(9, 2 * hidden, 2 * hidden),
            gru_candidate.reshape(9, 2 * hidden, hidden),
        ),
        scratch=[
            pltpu.VMEM((local + beyond, hidden), bf16),
            pltpu.VMEM((local + beyond + 2 * width, 6 * hidden), bf16),
        ],
        flops=2 * (local + beyond) * 9 * 2 * hidden * 3 * hidden * ITERS,
    )
    track_out = call(
        output_body,
        jax.ShapeDtypeStruct((half, channels), bf16),
        (returned.reshape(half, channels), local_tokens, time_out),
        flops=2 * half * channels * channels,
    )
    return refined.reshape(gru_state.shape), track_out[None]


def solution(mesh):
    placed = (
        P(("clip", "frame"), "band", None, None),
        P(("clip", "frame"), "band", None, None),
        P(("clip", "frame"), "band", None),
        P(("clip", "frame"), "band"),
        P(("clip", "band")),
        P(),
        P(),
        P(),
        P(),
        P(),
        P(),
        P(),
        P(),
        P(),
        P(),
    )
    return jax.shard_map(
        on_device,
        mesh=mesh,
        in_specs=placed,
        out_specs=(P(("clip", "frame"), "band", None, None), P(("clip", "frame"), "band", None)),
        check_vma=False,
    )
```

```python
import jax
import jax.numpy as jnp
from jax import lax
from jax.experimental import pallas as pl
from jax.experimental.pallas import tpu as pltpu
from jax.sharding import PartitionSpec as P

HEADS = 8
ITERS = 2
LANES = 128
MASK_ROWS = 16
HIDDEN = -1e30
LOG2E = 1.4426950408889634

f32 = jnp.float32
bf16 = jnp.bfloat16
VMEM = pl.BlockSpec(memory_space=pltpu.VMEM)
HBM = pl.BlockSpec(memory_space=pltpu.HBM)
LATER = pl.BlockSpec(memory_space=pl.ANY)


def dot(a, b):
    return jnp.dot(a, b, preferred_element_type=f32)


def call(body, out, near, scratch=(), flops=0, after=(), raw=(), grant=24 * 2**20, place=VMEM):
    args = (*raw, *near)
    return pl.pallas_call(
        lambda *refs: body(*refs[len(after) :]),
        out_shape=out,
        in_specs=[LATER] * len(after) + [HBM] * len(raw) + [VMEM] * len(near),
        out_specs=jax.tree.map(lambda _: place, out),
        scratch_shapes=scratch,
        compiler_params=pltpu.CompilerParams(vmem_limit_bytes=grant),
        cost_estimate=pl.CostEstimate(
            flops=flops,
            bytes_accessed=sum(x.size * x.dtype.itemsize for x in args),
            transcendentals=0,
        ),
    )(*after, *args)


def turned(slot, frames):
    return (slot + frames // 2) % frames


def exchange(x):
    frames = lax.axis_size("frame")
    return lax.all_to_all(
        x,
        "frame",
        split_axis=0,
        concat_axis=0,
        tiled=True,
        axis_index_groups=[[turned(i, frames) for i in range(frames)]],
    )


def pack_body(tokens, visible, out, flags, packed, sems):
    frames, rows, _ = out.shape
    share = tokens.shape[1]
    chunks = 4
    step = frames // chunks
    first = pltpu.make_async_copy(visible, flags, sems.at[0])
    first.start()
    coming = []
    for i in range(chunks):
        some = pl.ds(i * step, step)
        coming.append(
            [
                pltpu.make_async_copy(
                    tokens.at[pl.ds(turned(i * step, frames), step), :, pl.ds(c * LANES, LANES)],
                    packed.at[some, pl.ds(c * share, share), :],
                    sems.at[1 + 2 * i + c],
                )
                for c in range(2)
            ]
        )
    for copies in coming:
        for copy in copies:
            copy.start()
    first.wait()
    for g in range(frames):
        group = flags[turned(g, frames) * share // LANES, :].astype(f32)
        packed[g, 2 * share :, :] = jnp.broadcast_to(group[None], (MASK_ROWS, LANES)).astype(bf16)
    going = []
    for i, copies in enumerate(coming):
        for copy in copies:
            copy.wait()
        some = pl.ds(i * step, step)
        going.append(pltpu.make_async_copy(packed.at[some], out.at[some], sems.at[1 + 2 * chunks + i]))
        going[-1].start()
    for copy in going:
        copy.wait()


def project_body(
    pixels, tokens, w_query, w_key, w_value, w_time_query, w_time_key, w_time_value, query, key, value, w_time
):
    query[...] = dot(pixels[...], w_query[...]).astype(bf16)
    key[...] = dot(tokens[...], w_key[...]).astype(bf16)
    value[...] = dot(tokens[...], w_value[...]).astype(bf16)
    channels = w_time_query.shape[0]
    for i, weight in enumerate((w_time_query, w_time_key, w_time_value)):
        w_time[i * channels : (i + 1) * channels, :] = weight[...].astype(f32).T.astype(bf16)


def attend_body(
    query, key, value, other, visible, flags, w_key, w_value, w_out, state, context, edge
):
    channels = query.shape[1]
    head_dim = channels // HEADS
    keys = jnp.concatenate([key[...], dot(other[...], w_key[...]).astype(bf16)], axis=0)
    values = jnp.concatenate([value[...], dot(other[...], w_value[...]).astype(bf16)], axis=0)
    tracks = keys.shape[0]
    seen = jnp.concatenate([visible[...], flags[...]], axis=1).astype(f32)
    seen = [seen[:, i * LANES : (i + 1) * LANES] for i in range(tracks // LANES)]
    seen = jnp.concatenate(seen, axis=0).T
    seen = jnp.concatenate([seen[:, i : i + 1] for i in range(tracks // LANES)], axis=0)
    bias = jnp.where(seen > 0.5, 0.0, HIDDEN).astype(bf16)
    lane = lax.broadcasted_iota(jnp.int32, (1, LANES), 1)
    one = jnp.ones((1, 1), bf16)
    scale = LOG2E * head_dim**-0.5
    attended = []
    for tile in range(channels // LANES):
        some = slice(tile * LANES, (tile + 1) * LANES)
        spares = (0, LANES - 1)
        key_of = {x: jnp.where(lane == x, bias, keys[:, some]) for x in spares}
        value_of = {x: jnp.where(lane == x, one, values[:, some]) for x in spares}
        result = jnp.zeros((query.shape[0], LANES), f32)
        for head in range(LANES // head_dim):
            mine = lane // head_dim == head
            spare = spares[0] if head else spares[1]
            asking = jnp.where(mine, query[:, some], jnp.where(lane == spare, one, 0 * one))
            scores = lax.dot_general(
                asking, key_of[spare], (((1,), (1,)), ((), ())), preferred_element_type=f32
            )
            top = jnp.max(scores, axis=1, keepdims=True)
            weights = jnp.exp2((scores - top) * scale).astype(bf16)
            summed = dot(weights, value_of[spare])
            total = summed[:, spare : spare + 1]
            result = jnp.where(mine, summed * (1.0 / total), result)
        attended.append(result.astype(bf16))
    context[...] = dot(jnp.concatenate(attended, axis=1), w_out[...]).astype(bf16)
    count = edge.shape[0]
    start = pl.multiple_of((1 - lax.axis_index("band")) * (query.shape[0] - count), count)
    edge[:, :LANES] = state[pl.ds(start, count), :]
    edge[:, LANES:] = context[pl.ds(start, count), :]


def temporal_body(packed, query_frame, w_all, out, result, sems):
    frames, share, channels = out.shape
    head_dim = channels // HEADS
    tiles = frames * share // LANES
    beside = LANES // share
    me = lax.axis_index("frame")
    piece = lax.broadcasted_iota(jnp.int32, (1, LANES), 1) // share

    def fold(x, add=jnp.add):
        shift = share
        while shift < LANES:
            x = add(x, pltpu.roll(x, shift, 1))
            shift *= 2
        return x

    def everywhere(x, which):
        return fold(jnp.where(piece == which, x, 0.0))

    asked = query_frame[pl.ds(me * share // LANES, 1), :].astype(f32)
    asked = everywhere(asked, me % beside)
    flags = everywhere(packed[:, 2 * share, :].astype(f32), me % beside)
    seen = []
    for tile in range(tiles):
        row = jnp.zeros((1, LANES), f32)
        for o in range(beside):
            g = tile * beside + o
            row = jnp.where(piece == o, flags[g : g + 1, :], row)
        seen.append(row > 0.5)

    left = packed[:, :share, :].reshape(frames * share, LANES)
    right = packed[:, share : 2 * share, :].reshape(frames * share, LANES)
    rows = jnp.concatenate([left, right], axis=1)
    projected = lax.dot_general(
        w_all[...], rows, (((1,), (1,)), ((), ())), preferred_element_type=f32
    )
    projected = projected.astype(bf16).astype(f32)
    query, key, value = (
        [
            projected[i * channels : (i + 1) * channels, t * LANES : (t + 1) * LANES]
            for t in range(tiles)
        ]
        for i in range(3)
    )
    anchor = jnp.zeros((channels, LANES), f32)
    for tile in range(tiles):
        frame = turned(piece + tile * beside, frames).astype(f32)
        anchor = anchor + jnp.where(asked == frame, query[tile], 0.0)
    anchor = fold(anchor)

    copies = []
    for tile in range(tiles):
        attended = jnp.zeros((channels, LANES), f32)
        for o in range(beside):
            joint = (everywhere(query[tile], o) + anchor).astype(bf16).astype(f32)
            scores = []
            for other in range(tiles):
                product = (key[other] * joint).reshape(HEADS, head_dim, LANES)
                score = jnp.sum(product, axis=1) * head_dim**-0.5
                scores.append(jnp.where(seen[other], score, HIDDEN))
            top = scores[0]
            for score in scores[1:]:
                top = jnp.maximum(top, score)
            top = fold(top, jnp.maximum)
            raised = [jnp.exp(score - top) for score in scores]
            total = fold(sum(raised[1:], raised[0]))
            summed = jnp.zeros((HEADS, head_dim, LANES), f32)
            for other in range(tiles):
                weight = (raised[other] / total).astype(bf16).astype(f32)
                here = value[other].reshape(HEADS, head_dim, LANES)
                summed = summed + here * weight[:, None, :]
            summed = fold(summed.reshape(channels, LANES))
            attended = jnp.where(piece == o, summed, attended)
        some = pl.ds(tile * beside, beside)
        result[some] = attended.T.astype(bf16).reshape(beside, share, channels)
        copies.append(pltpu.make_async_copy(result.at[some], out.at[some], sems.at[tile]))
        copies[-1].start()
    for copy in copies:
        copy.wait()


def refine_body(state, context, halo, w_gates, w_cand, out, field, wide):
    taps, both, _ = w_gates.shape
    local, hidden = state.shape
    beyond = halo.shape[0]
    pixels = local + beyond
    width = (wide.shape[0] - pixels) // 2
    band = lax.axis_index("band")
    here = pl.multiple_of(band * beyond, beyond)
    there = pl.multiple_of((1 - band) * local, beyond)
    col = lax.broadcasted_iota(jnp.int32, (pixels, hidden), 0) % width
    wide[:width, :] = jnp.zeros((width, 3 * both), bf16)
    wide[width + pixels :, :] = jnp.zeros((width, 3 * both), bf16)

    def spread(values, lane):
        before = jnp.where(col == 0, 0.0, pltpu.roll(values, 1, 0))
        after = jnp.where(col == width - 1, 0.0, pltpu.roll(values, pixels - 1, 0))
        for c, shifted in enumerate((before, values, after)):
            first = c * both + lane
            wide[width : width + pixels, first : first + hidden] = shifted.astype(bf16)

    def conv(weight):
        rows = [wide[r * width : r * width + pixels, :] for r in range(3)]
        return dot(jnp.concatenate(rows, axis=1), weight[...].reshape(taps * both, -1))

    field[pl.ds(here, local), :] = context[...]
    field[pl.ds(there, beyond), :] = halo[:, hidden:]
    spread(field[...].astype(f32), hidden)
    field[pl.ds(here, local), :] = state[...]
    field[pl.ds(there, beyond), :] = halo[:, :hidden]
    now = field[...].astype(f32)
    for _ in range(ITERS):
        spread(now, 0)
        gates = conv(w_gates)
        update = jax.nn.sigmoid(gates[:, :hidden])
        reset = jax.nn.sigmoid(gates[:, hidden:])
        spread((reset * now).astype(bf16).astype(f32), 0)
        cand = jnp.tanh(conv(w_cand))
        now = ((1.0 - update) * now + update * cand).astype(bf16).astype(f32)
    field[...] = now.astype(bf16)
    out[...] = field[pl.ds(here, local), :]


def output_body(returned, tokens, w_out, out):
    rows = returned.shape[0] // 2
    for i in range(2):
        mine = slice(turned(i, 2) * rows, (turned(i, 2) + 1) * rows)
        added = dot(returned[i * rows : (i + 1) * rows, :], w_out[...])
        out[mine, :] = (tokens[mine, :].astype(f32) + added).astype(bf16)


def on_device(
    pixels,
    gru_state,
    tokens,
    visible,
    query_frame,
    pixel_query,
    pixel_key,
    pixel_value,
    pixel_out,
    time_query,
    time_key,
    time_value,
    time_out,
    gru_gates,
    gru_candidate,
):
    frames = lax.axis_size("frame")
    _, band_rows, width, channels = pixels.shape
    hidden = gru_state.shape[3]
    half = tokens.shape[1]
    share = half // frames
    local = band_rows * width
    beyond = 2 * ITERS * width
    assert LANES % share == 0
    assert lax.axis_size("band") == 2 and channels == 2 * LANES and hidden == LANES
    swap = [(0, 1), (1, 0)]
    local_tokens = tokens[0]
    flat_state = gru_state.reshape(local, hidden)
    groups = half // LANES

    other = lax.ppermute(local_tokens, "band", swap)
    flags = lax.ppermute(visible, "band", swap)
    packed = call(
        pack_body,
        jax.ShapeDtypeStruct((frames, 2 * share + MASK_ROWS, LANES), bf16),
        (),
        scratch=[
            pltpu.VMEM((groups, LANES), jnp.int32),
            pltpu.VMEM((frames, 2 * share + MASK_ROWS, LANES), bf16),
            pltpu.SemaphoreType.DMA((13,)),
        ],
        raw=(local_tokens.reshape(frames, share, channels), visible.reshape(groups, LANES)),
        flops=10**10,
        grant=60 * 2**20,
        place=HBM,
    )
    arrived = exchange(packed)

    query, key, value, w_time = call(
        project_body,
        (
            jax.ShapeDtypeStruct((local, channels), bf16),
            jax.ShapeDtypeStruct((half, channels), bf16),
            jax.ShapeDtypeStruct((half, channels), bf16),
            jax.ShapeDtypeStruct((3 * channels, channels), bf16),
        ),
        (
            pixels.reshape(local, channels),
            local_tokens,
            pixel_query,
            pixel_key,
            pixel_value,
            time_query,
            time_key,
            time_value,
        ),
        flops=2 * (local + 2 * half) * channels * channels,
    )
    context, edge = call(
        attend_body,
        (
            jax.ShapeDtypeStruct((local, hidden), bf16),
            jax.ShapeDtypeStruct((beyond, 2 * hidden), bf16),
        ),
        (query, key, value, other, visible, flags, pixel_key, pixel_value, pixel_out, flat_state),
        flops=4 * local * 2 * half * channels * HEADS,
    )
    halo = lax.ppermute(edge, "band", swap)

    attended = call(
        temporal_body,
        jax.ShapeDtypeStruct((frames, share, channels), bf16),
        (arrived, query_frame.reshape(groups, LANES), w_time),
        after=(edge,),
        scratch=[
            pltpu.VMEM((frames, share, channels), bf16),
            pltpu.SemaphoreType.DMA((frames,)),
        ],
        place=HBM,
        flops=6 * half * channels * channels * 4,
    )
    returned = exchange(attended)

    refined = call(
        refine_body,
        jax.ShapeDtypeStruct((local, hidden), bf16),
        (
            flat_state,
            context,
            halo,
            gru_gates.reshape(9, 2 * hidden, 2 * hidden),
            gru_candidate.reshape(9, 2 * hidden, hidden),
        ),
        scratch=[
            pltpu.VMEM((local + beyond, hidden), bf16),
            pltpu.VMEM((local + beyond + 2 * width, 6 * hidden), bf16),
        ],
        flops=2 * (local + beyond) * 9 * 2 * hidden * 3 * hidden * ITERS,
    )
    track_out = call(
        output_body,
        jax.ShapeDtypeStruct((half, channels), bf16),
        (returned.reshape(half, channels), local_tokens, time_out),
        flops=2 * half * channels * channels,
    )
    return refined.reshape(gru_state.shape), track_out[None]


def solution(mesh):
    placed = (
        P(("clip", "frame"), "band", None, None),
        P(("clip", "frame"), "band", None, None),
        P(("clip", "frame"), "band", None),
        P(("clip", "frame"), "band"),
        P(("clip", "band")),
        P(),
        P(),
        P(),
        P(),
        P(),
        P(),
        P(),
        P(),
        P(),
        P(),
    )
    return jax.shard_map(
        on_device,
        mesh=mesh,
        in_specs=placed,
        out_specs=(P(("clip", "frame"), "band", None, None), P(("clip", "frame"), "band", None)),
        check_vma=False,
    )
```

```python
import jax
import jax.numpy as jnp
from jax import lax
from jax.experimental import pallas as pl
from jax.experimental.pallas import tpu as pltpu
from jax.sharding import PartitionSpec as P

HEADS = 8
ITERS = 2
LANES = 128
MASK_ROWS = 8
HIDDEN = -1e30
LOG2E = 1.4426950408889634

f32 = jnp.float32
bf16 = jnp.bfloat16
VMEM = pl.BlockSpec(memory_space=pltpu.VMEM)
HBM = pl.BlockSpec(memory_space=pltpu.HBM)
LATER = pl.BlockSpec(memory_space=pl.ANY)


def dot(a, b):
    return jnp.dot(a, b, preferred_element_type=f32)


def call(body, out, near, scratch=(), flops=0, after=(), raw=(), grant=24 * 2**20, place=VMEM):
    args = (*raw, *near)
    return pl.pallas_call(
        lambda *refs: body(*refs[len(after) :]),
        out_shape=out,
        in_specs=[LATER] * len(after) + [HBM] * len(raw) + [VMEM] * len(near),
        out_specs=jax.tree.map(lambda _: place, out),
        scratch_shapes=scratch,
        compiler_params=pltpu.CompilerParams(vmem_limit_bytes=grant),
        cost_estimate=pl.CostEstimate(
            flops=flops,
            bytes_accessed=sum(x.size * x.dtype.itemsize for x in args),
            transcendentals=0,
        ),
    )(*after, *args)


def turned(slot, frames):
    return (slot + frames // 2) % frames


def exchange(x):
    frames = lax.axis_size("frame")
    return lax.all_to_all(
        x,
        "frame",
        split_axis=0,
        concat_axis=0,
        tiled=True,
        axis_index_groups=[[turned(i, frames) for i in range(frames)]],
    )


def pack_body(tokens, visible, out, flags, packed, sems):
    frames, rows, _ = out.shape
    share = tokens.shape[1]
    chunks = 4
    step = frames // chunks
    first = pltpu.make_async_copy(visible, flags, sems.at[0])
    first.start()
    coming = []
    for i in range(chunks):
        some = pl.ds(i * step, step)
        coming.append(
            [
                pltpu.make_async_copy(
                    tokens.at[pl.ds(turned(i * step, frames), step), :, pl.ds(c * LANES, LANES)],
                    packed.at[some, pl.ds(c * share, share), :],
                    sems.at[1 + 2 * i + c],
                )
                for c in range(2)
            ]
        )
    for copies in coming:
        for copy in copies:
            copy.start()
    first.wait()
    for g in range(frames):
        group = flags[turned(g, frames) * share // LANES, :].astype(f32)
        packed[g, 2 * share :, :] = jnp.broadcast_to(group[None], (MASK_ROWS, LANES)).astype(bf16)
    going = []
    for i, copies in enumerate(coming):
        for copy in copies:
            copy.wait()
        some = pl.ds(i * step, step)
        going.append(pltpu.make_async_copy(packed.at[some], out.at[some], sems.at[1 + 2 * chunks + i]))
        going[-1].start()
    for copy in going:
        copy.wait()


def project_body(
    pixels, tokens, w_query, w_key, w_value, w_time_query, w_time_key, w_time_value, query, key, value, w_time
):
    query[...] = dot(pixels[...], w_query[...]).astype(bf16)
    key[...] = dot(tokens[...], w_key[...]).astype(bf16)
    value[...] = dot(tokens[...], w_value[...]).astype(bf16)
    channels = w_time_query.shape[0]
    for i, weight in enumerate((w_time_query, w_time_key, w_time_value)):
        w_time[i * channels : (i + 1) * channels, :] = weight[...].astype(f32).T.astype(bf16)


def attend_body(
    query, key, value, other, visible, flags, w_key, w_value, w_out, state, context, edge
):
    channels = query.shape[1]
    head_dim = channels // HEADS
    keys = jnp.concatenate([key[...], dot(other[...], w_key[...]).astype(bf16)], axis=0)
    values = jnp.concatenate([value[...], dot(other[...], w_value[...]).astype(bf16)], axis=0)
    tracks = keys.shape[0]
    seen = jnp.concatenate([visible[...], flags[...]], axis=1).astype(f32)
    seen = [seen[:, i * LANES : (i + 1) * LANES] for i in range(tracks // LANES)]
    seen = jnp.concatenate(seen, axis=0).T
    seen = jnp.concatenate([seen[:, i : i + 1] for i in range(tracks // LANES)], axis=0)
    bias = jnp.where(seen > 0.5, 0.0, HIDDEN).astype(bf16)
    lane = lax.broadcasted_iota(jnp.int32, (1, LANES), 1)
    one = jnp.ones((1, 1), bf16)
    scale = LOG2E * head_dim**-0.5
    attended = []
    for tile in range(channels // LANES):
        some = slice(tile * LANES, (tile + 1) * LANES)
        spares = (0, LANES - 1)
        key_of = {x: jnp.where(lane == x, bias, keys[:, some]) for x in spares}
        value_of = {x: jnp.where(lane == x, one, values[:, some]) for x in spares}
        result = jnp.zeros((query.shape[0], LANES), f32)
        for head in range(LANES // head_dim):
            mine = lane // head_dim == head
            spare = spares[0] if head else spares[1]
            asking = jnp.where(mine, query[:, some], jnp.where(lane == spare, one, 0 * one))
            scores = lax.dot_general(
                asking, key_of[spare], (((1,), (1,)), ((), ())), preferred_element_type=f32
            )
            top = jnp.max(scores, axis=1, keepdims=True)
            weights = jnp.exp2((scores - top) * scale).astype(bf16)
            summed = dot(weights, value_of[spare])
            total = summed[:, spare : spare + 1]
            result = jnp.where(mine, summed * (1.0 / total), result)
        attended.append(result.astype(bf16))
    context[...] = dot(jnp.concatenate(attended, axis=1), w_out[...]).astype(bf16)
    count = edge.shape[0]
    start = pl.multiple_of((1 - lax.axis_index("band")) * (query.shape[0] - count), count)
    edge[:, :LANES] = state[pl.ds(start, count), :]
    edge[:, LANES:] = context[pl.ds(start, count), :]


def temporal_body(packed, query_frame, w_all, out, result, sems):
    frames, share, channels = out.shape
    head_dim = channels // HEADS
    tiles = frames * share // LANES
    beside = LANES // share
    me = lax.axis_index("frame")
    piece = lax.broadcasted_iota(jnp.int32, (1, LANES), 1) // share

    def fold(x, add=jnp.add):
        shift = share
        while shift < LANES:
            x = add(x, pltpu.roll(x, shift, 1))
            shift *= 2
        return x

    def everywhere(x, which):
        return fold(jnp.where(piece == which, x, 0.0))

    asked = query_frame[pl.ds(me * share // LANES, 1), :].astype(f32)
    asked = everywhere(asked, me % beside)
    flags = everywhere(packed[:, 2 * share, :].astype(f32), me % beside)
    seen = []
    for tile in range(tiles):
        row = jnp.zeros((1, LANES), f32)
        for o in range(beside):
            g = tile * beside + o
            row = jnp.where(piece == o, flags[g : g + 1, :], row)
        seen.append(row > 0.5)

    left = packed[:, :share, :].reshape(frames * share, LANES)
    right = packed[:, share : 2 * share, :].reshape(frames * share, LANES)
    rows = jnp.concatenate([left, right], axis=1)
    projected = lax.dot_general(
        w_all[...], rows, (((1,), (1,)), ((), ())), preferred_element_type=f32
    )
    projected = projected.astype(bf16).astype(f32)
    query, key, value = (
        [
            projected[i * channels : (i + 1) * channels, t * LANES : (t + 1) * LANES]
            for t in range(tiles)
        ]
        for i in range(3)
    )
    anchor = jnp.zeros((channels, LANES), f32)
    for tile in range(tiles):
        frame = turned(piece + tile * beside, frames).astype(f32)
        anchor = anchor + jnp.where(asked == frame, query[tile], 0.0)
    anchor = fold(anchor)

    copies = []
    for tile in range(tiles):
        attended = jnp.zeros((channels, LANES), f32)
        for o in range(beside):
            joint = (everywhere(query[tile], o) + anchor).astype(bf16).astype(f32)
            scores = []
            for other in range(tiles):
                product = (key[other] * joint).reshape(HEADS, head_dim, LANES)
                score = jnp.sum(product, axis=1) * head_dim**-0.5
                scores.append(jnp.where(seen[other], score, HIDDEN))
            top = scores[0]
            for score in scores[1:]:
                top = jnp.maximum(top, score)
            top = fold(top, jnp.maximum)
            raised = [jnp.exp(score - top) for score in scores]
            total = fold(sum(raised[1:], raised[0]))
            summed = jnp.zeros((HEADS, head_dim, LANES), f32)
            for other in range(tiles):
                weight = (raised[other] / total).astype(bf16).astype(f32)
                here = value[other].reshape(HEADS, head_dim, LANES)
                summed = summed + here * weight[:, None, :]
            summed = fold(summed.reshape(channels, LANES))
            attended = jnp.where(piece == o, summed, attended)
        some = pl.ds(tile * beside, beside)
        result[some] = attended.T.astype(bf16).reshape(beside, share, channels)
        copies.append(pltpu.make_async_copy(result.at[some], out.at[some], sems.at[tile]))
        copies[-1].start()
    for copy in copies:
        copy.wait()


def refine_body(state, context, halo, w_gates, w_cand, out, field, fresh, wide):
    taps, both, _ = w_gates.shape
    local, hidden = state.shape
    beyond = halo.shape[0]
    pixels = local + beyond
    width = (wide.shape[0] - pixels) // 2
    band = lax.axis_index("band")
    here = pl.multiple_of(band * beyond, beyond)
    there = pl.multiple_of((1 - band) * local, beyond)
    col = lax.broadcasted_iota(jnp.int32, (pixels, hidden), 0) % width
    wide[:width, :] = jnp.zeros((width, 3 * both), bf16)
    wide[width + pixels :, :] = jnp.zeros((width, 3 * both), bf16)

    def window(k, below=0):
        start = pl.multiple_of(band * k * width, width) + below * width
        return pl.ds(pl.multiple_of(start, width), pixels - k * width)

    def spread(values, lane, k):
        count = values.shape[0]
        before = jnp.where(col[:count] == 0, 0.0, pltpu.roll(values, 1, 0))
        after = jnp.where(col[:count] == width - 1, 0.0, pltpu.roll(values, count - 1, 0))
        for c, shifted in enumerate((before, values, after)):
            first = c * both + lane
            wide[window(k, 1), first : first + hidden] = shifted.astype(bf16)

    def conv(weight, k):
        rows = [wide[window(k, r), :] for r in range(3)]
        return dot(jnp.concatenate(rows, axis=1), weight[...].reshape(taps * both, -1))

    field[pl.ds(here, local), :] = context[...].astype(f32)
    field[pl.ds(there, beyond), :] = halo[:, hidden:].astype(f32)
    spread(field[...], hidden, 0)
    field[pl.ds(here, local), :] = state[...].astype(f32)
    field[pl.ds(there, beyond), :] = halo[:, :hidden].astype(f32)
    spread(field[...], 0, 0)
    for k in range(1, 2 * ITERS, 2):
        gates = conv(w_gates, k)
        fresh[window(k), :] = jax.nn.sigmoid(gates[:, :hidden])
        reset = jax.nn.sigmoid(gates[:, hidden:])
        spread((reset * field[window(k), :]).astype(bf16).astype(f32), 0, k)
        cand = jnp.tanh(conv(w_cand, k + 1))
        update = fresh[window(k + 1), :]
        now = (1.0 - update) * field[window(k + 1), :] + update * cand
        if k + 1 < 2 * ITERS:
            now = now.astype(bf16).astype(f32)
            field[window(k + 1), :] = now
            spread(now, 0, k + 1)
    out[...] = now.astype(bf16)


def output_body(returned, tokens, w_out, out):
    rows = returned.shape[0] // 2
    for i in range(2):
        mine = slice(turned(i, 2) * rows, (turned(i, 2) + 1) * rows)
        added = dot(returned[i * rows : (i + 1) * rows, :], w_out[...])
        out[mine, :] = (tokens[mine, :].astype(f32) + added).astype(bf16)


def on_device(
    pixels,
    gru_state,
    tokens,
    visible,
    query_frame,
    pixel_query,
    pixel_key,
    pixel_value,
    pixel_out,
    time_query,
    time_key,
    time_value,
    time_out,
    gru_gates,
    gru_candidate,
):
    frames = lax.axis_size("frame")
    _, band_rows, width, channels = pixels.shape
    hidden = gru_state.shape[3]
    half = tokens.shape[1]
    share = half // frames
    local = band_rows * width
    beyond = 2 * ITERS * width
    assert LANES % share == 0
    assert lax.axis_size("band") == 2 and channels == 2 * LANES and hidden == LANES
    swap = [(0, 1), (1, 0)]
    local_tokens = tokens[0]
    flat_state = gru_state.reshape(local, hidden)
    groups = half // LANES

    other = lax.ppermute(local_tokens, "band", swap)
    flags = lax.ppermute(visible, "band", swap)
    packed = call(
        pack_body,
        jax.ShapeDtypeStruct((frames, 2 * share + MASK_ROWS, LANES), bf16),
        (),
        scratch=[
            pltpu.VMEM((groups, LANES), jnp.int32),
            pltpu.VMEM((frames, 2 * share + MASK_ROWS, LANES), bf16),
            pltpu.SemaphoreType.DMA((13,)),
        ],
        raw=(local_tokens.reshape(frames, share, channels), visible.reshape(groups, LANES)),
        flops=10**10,
        grant=60 * 2**20,
        place=HBM,
    )
    arrived = exchange(packed)

    query, key, value, w_time = call(
        project_body,
        (
            jax.ShapeDtypeStruct((local, channels), bf16),
            jax.ShapeDtypeStruct((half, channels), bf16),
            jax.ShapeDtypeStruct((half, channels), bf16),
            jax.ShapeDtypeStruct((3 * channels, channels), bf16),
        ),
        (
            pixels.reshape(local, channels),
            local_tokens,
            pixel_query,
            pixel_key,
            pixel_value,
            time_query,
            time_key,
            time_value,
        ),
        flops=2 * (local + 2 * half) * channels * channels,
    )
    context, edge = call(
        attend_body,
        (
            jax.ShapeDtypeStruct((local, hidden), bf16),
            jax.ShapeDtypeStruct((beyond, 2 * hidden), bf16),
        ),
        (query, key, value, other, visible, flags, pixel_key, pixel_value, pixel_out, flat_state),
        flops=4 * local * 2 * half * channels * HEADS,
    )
    halo = lax.ppermute(edge, "band", swap)

    attended = call(
        temporal_body,
        jax.ShapeDtypeStruct((frames, share, channels), bf16),
        (arrived, query_frame.reshape(groups, LANES), w_time),
        after=(edge,),
        scratch=[
            pltpu.VMEM((frames, share, channels), bf16),
            pltpu.SemaphoreType.DMA((frames,)),
        ],
        place=HBM,
        flops=6 * half * channels * channels * 4,
    )
    returned = exchange(attended)

    refined = call(
        refine_body,
        jax.ShapeDtypeStruct((local, hidden), bf16),
        (
            flat_state,
            context,
            halo,
            gru_gates.reshape(9, 2 * hidden, 2 * hidden),
            gru_candidate.reshape(9, 2 * hidden, hidden),
        ),
        scratch=[
            pltpu.VMEM((local + beyond, hidden), f32),
            pltpu.VMEM((local + beyond, hidden), f32),
            pltpu.VMEM((local + beyond + 2 * width, 6 * hidden), bf16),
        ],
        flops=2 * (local + beyond) * 9 * 2 * hidden * 3 * hidden * ITERS,
    )
    track_out = call(
        output_body,
        jax.ShapeDtypeStruct((half, channels), bf16),
        (returned.reshape(half, channels), local_tokens, time_out),
        flops=2 * half * channels * channels,
    )
    return refined.reshape(gru_state.shape), track_out[None]


def solution(mesh):
    placed = (
        P(("clip", "frame"), "band", None, None),
        P(("clip", "frame"), "band", None, None),
        P(("clip", "frame"), "band", None),
        P(("clip", "frame"), "band"),
        P(("clip", "band")),
        P(),
        P(),
        P(),
        P(),
        P(),
        P(),
        P(),
        P(),
        P(),
        P(),
    )
    return jax.shard_map(
        on_device,
        mesh=mesh,
        in_specs=placed,
        out_specs=(P(("clip", "frame"), "band", None, None), P(("clip", "frame"), "band", None)),
        check_vma=False,
    )
```

```python
import jax
import jax.numpy as jnp
from jax import lax
from jax.experimental import pallas as pl
from jax.experimental.pallas import tpu as pltpu
from jax.sharding import PartitionSpec as P

HEADS = 8
ITERS = 2
LANES = 128
MASK_ROWS = 8
HIDDEN = -1e30
LOG2E = 1.4426950408889634

f32 = jnp.float32
bf16 = jnp.bfloat16
VMEM = pl.BlockSpec(memory_space=pltpu.VMEM)
HBM = pl.BlockSpec(memory_space=pltpu.HBM)
LATER = pl.BlockSpec(memory_space=pl.ANY)


def dot(a, b):
    return jnp.dot(a, b, preferred_element_type=f32)


def call(body, out, near, scratch=(), flops=0, after=(), raw=(), grant=24 * 2**20, place=VMEM):
    args = (*raw, *near)
    return pl.pallas_call(
        lambda *refs: body(*refs[len(after) :]),
        out_shape=out,
        in_specs=[LATER] * len(after) + [HBM] * len(raw) + [VMEM] * len(near),
        out_specs=jax.tree.map(lambda _: place, out),
        scratch_shapes=scratch,
        compiler_params=pltpu.CompilerParams(vmem_limit_bytes=grant),
        cost_estimate=pl.CostEstimate(
            flops=flops,
            bytes_accessed=sum(x.size * x.dtype.itemsize for x in args),
            transcendentals=0,
        ),
    )(*after, *args)


def turned(slot, frames):
    return (slot + frames // 2) % frames


def exchange(x):
    frames = lax.axis_size("frame")
    return lax.all_to_all(
        x,
        "frame",
        split_axis=0,
        concat_axis=0,
        tiled=True,
        axis_index_groups=[[turned(i, frames) for i in range(frames)]],
    )


def pack_body(tokens, visible, out, flags, packed, sems):
    frames, rows, _ = out.shape
    share = tokens.shape[1]
    chunks = 4
    step = frames // chunks
    first = pltpu.make_async_copy(visible, flags, sems.at[0])
    first.start()
    coming = []
    for i in range(chunks):
        some = pl.ds(i * step, step)
        coming.append(
            [
                pltpu.make_async_copy(
                    tokens.at[pl.ds(turned(i * step, frames), step), :, pl.ds(c * LANES, LANES)],
                    packed.at[some, pl.ds(c * share, share), :],
                    sems.at[1 + 2 * i + c],
                )
                for c in range(2)
            ]
        )
    for copies in coming:
        for copy in copies:
            copy.start()
    first.wait()
    for g in range(frames):
        group = flags[turned(g, frames) * share // LANES, :].astype(f32)
        packed[g, 2 * share :, :] = jnp.broadcast_to(group[None], (MASK_ROWS, LANES)).astype(bf16)
    going = []
    for i, copies in enumerate(coming):
        for copy in copies:
            copy.wait()
        some = pl.ds(i * step, step)
        going.append(pltpu.make_async_copy(packed.at[some], out.at[some], sems.at[1 + 2 * chunks + i]))
        going[-1].start()
    for copy in going:
        copy.wait()


def project_body(
    pixels,
    tokens,
    w_query,
    w_key,
    w_value,
    w_time_query,
    w_time_key,
    w_time_value,
    w_time_out,
    query,
    key,
    value,
    w_time,
    w_out,
):
    query[...] = dot(pixels[...], w_query[...]).astype(bf16)
    key[...] = dot(tokens[...], w_key[...]).astype(bf16)
    value[...] = dot(tokens[...], w_value[...]).astype(bf16)
    channels = w_time_out.shape[0]
    line = lax.broadcasted_iota(jnp.int32, (channels, channels), 0)
    column = lax.broadcasted_iota(jnp.int32, (channels, channels), 1)
    order = line % HEADS * (channels // HEADS) + line // HEADS
    order = jnp.where(column == order, 1.0, 0.0).astype(bf16)
    for i, weight in enumerate((w_time_query, w_time_key, w_time_value)):
        moved = lax.dot_general(
            order, weight[...], (((1,), (1,)), ((), ())), preferred_element_type=f32
        )
        w_time[i * channels : (i + 1) * channels, :] = moved.astype(bf16)
    w_out[...] = dot(order, w_time_out[...]).astype(bf16)


def attend_body(
    query, key, value, other, visible, flags, w_key, w_value, w_out, state, context, edge
):
    channels = query.shape[1]
    head_dim = channels // HEADS
    keys = jnp.concatenate([key[...], dot(other[...], w_key[...]).astype(bf16)], axis=0)
    values = jnp.concatenate([value[...], dot(other[...], w_value[...]).astype(bf16)], axis=0)
    tracks = keys.shape[0]
    seen = jnp.concatenate([visible[...], flags[...]], axis=1).astype(f32)
    seen = [seen[:, i * LANES : (i + 1) * LANES] for i in range(tracks // LANES)]
    seen = jnp.concatenate(seen, axis=0).T
    seen = jnp.concatenate([seen[:, i : i + 1] for i in range(tracks // LANES)], axis=0)
    bias = jnp.where(seen > 0.5, 0.0, HIDDEN).astype(bf16)
    lane = lax.broadcasted_iota(jnp.int32, (1, LANES), 1)
    one = jnp.ones((1, 1), bf16)
    scale = LOG2E * head_dim**-0.5
    attended = []
    for tile in range(channels // LANES):
        some = slice(tile * LANES, (tile + 1) * LANES)
        spares = (0, LANES - 1)
        key_of = {x: jnp.where(lane == x, bias, keys[:, some]) for x in spares}
        value_of = {x: jnp.where(lane == x, one, values[:, some]) for x in spares}
        result = jnp.zeros((query.shape[0], LANES), f32)
        for head in range(LANES // head_dim):
            mine = lane // head_dim == head
            spare = spares[0] if head else spares[1]
            asking = jnp.where(mine, query[:, some], jnp.where(lane == spare, one, 0 * one))
            scores = lax.dot_general(
                asking, key_of[spare], (((1,), (1,)), ((), ())), preferred_element_type=f32
            )
            top = jnp.max(scores, axis=1, keepdims=True)
            weights = jnp.exp2((scores - top) * scale).astype(bf16)
            summed = dot(weights, value_of[spare])
            total = summed[:, spare : spare + 1]
            result = jnp.where(mine, summed * (1.0 / total), result)
        attended.append(result.astype(bf16))
    context[...] = dot(jnp.concatenate(attended, axis=1), w_out[...]).astype(bf16)
    count = edge.shape[0]
    start = pl.multiple_of((1 - lax.axis_index("band")) * (query.shape[0] - count), count)
    edge[:, :LANES] = state[pl.ds(start, count), :]
    edge[:, LANES:] = context[pl.ds(start, count), :]


def temporal_body(packed, query_frame, w_all, out, result, sems):
    frames, share, channels = out.shape
    head_dim = channels // HEADS
    tiles = frames * share // LANES
    beside = LANES // share
    me = lax.axis_index("frame")
    piece = lax.broadcasted_iota(jnp.int32, (1, LANES), 1) // share

    def fold(x, add=jnp.add):
        shift = share
        while shift < LANES:
            x = add(x, pltpu.roll(x, shift, 1))
            shift *= 2
        return x

    def everywhere(x, which):
        return fold(jnp.where(piece == which, x, 0.0))

    def apart(x):
        if beside == 2:
            other = pltpu.roll(x, share, 1)
            return [jnp.where(piece == 0, x, other), jnp.where(piece == 0, other, x)]
        return [everywhere(x, o) for o in range(beside)]

    def together(parts):
        if beside == 2:
            a, b = parts
            other = pltpu.roll(jnp.where(piece == 0, b, a), share, 1)
            return jnp.where(piece == 0, a, b) + other
        x = jnp.zeros_like(parts[0])
        for o, part in enumerate(parts):
            x = jnp.where(piece == o, fold(part), x)
        return x

    asked = query_frame[pl.ds(me * share // LANES, 1), :].astype(f32)
    asked = everywhere(asked, me % beside)
    flags = everywhere(packed[:, 2 * share, :].astype(f32), me % beside)
    seen = []
    for tile in range(tiles):
        row = jnp.zeros((1, LANES), f32)
        for o in range(beside):
            g = tile * beside + o
            row = jnp.where(piece == o, flags[g : g + 1, :], row)
        seen.append(row > 0.5)

    left = packed[:, :share, :].reshape(frames * share, LANES)
    right = packed[:, share : 2 * share, :].reshape(frames * share, LANES)
    rows = jnp.concatenate([left, right], axis=1)
    projected = lax.dot_general(
        w_all[...], rows, (((1,), (1,)), ((), ())), preferred_element_type=f32
    )
    projected = projected.astype(bf16).astype(f32)
    query, key, value = (
        [
            projected[i * channels : (i + 1) * channels, t * LANES : (t + 1) * LANES]
            for t in range(tiles)
        ]
        for i in range(3)
    )
    anchor = jnp.zeros((channels, LANES), f32)
    for tile in range(tiles):
        frame = turned(piece + tile * beside, frames).astype(f32)
        anchor = anchor + jnp.where(asked == frame, query[tile], 0.0)
    anchor = fold(anchor)

    copies = []
    by_head = (head_dim, HEADS, LANES)
    for tile in range(tiles):
        parts = []
        for asking in apart(query[tile]):
            joint = (asking + anchor).astype(bf16).astype(f32)
            scores = []
            for other in range(tiles):
                product = (key[other] * joint).reshape(by_head)
                score = jnp.sum(product, axis=0) * head_dim**-0.5
                scores.append(jnp.where(seen[other], score, HIDDEN))
            top = scores[0]
            for score in scores[1:]:
                top = jnp.maximum(top, score)
            top = fold(top, jnp.maximum)
            raised = [jnp.exp(score - top) for score in scores]
            total = fold(sum(raised[1:], raised[0]))
            summed = None
            for other in range(tiles):
                weight = (raised[other] / total).astype(bf16).astype(f32)
                term = value[other].reshape(by_head) * weight[None]
                summed = term if summed is None else summed + term
            parts.append(summed.reshape(channels, LANES))
        some = pl.ds(tile * beside, beside)
        result[some] = together(parts).T.astype(bf16).reshape(beside, share, channels)
        copies.append(pltpu.make_async_copy(result.at[some], out.at[some], sems.at[tile]))
        copies[-1].start()
    for copy in copies:
        copy.wait()


def refine_body(state, context, halo, w_gates, w_cand, out, field, fresh, wide):
    taps, both, _ = w_gates.shape
    local, hidden = state.shape
    beyond = halo.shape[0]
    pixels = local + beyond
    width = (wide.shape[0] - pixels) // 2
    band = lax.axis_index("band")
    here = pl.multiple_of(band * beyond, beyond)
    there = pl.multiple_of((1 - band) * local, beyond)
    col = lax.broadcasted_iota(jnp.int32, (pixels, hidden), 0) % width
    wide[:width, :] = jnp.zeros((width, 3 * both), bf16)
    wide[width + pixels :, :] = jnp.zeros((width, 3 * both), bf16)

    def window(k, below=0):
        start = pl.multiple_of(band * k * width, width) + below * width
        return pl.ds(pl.multiple_of(start, width), pixels - k * width)

    def spread(values, lane, k):
        count = values.shape[0]
        before = jnp.where(col[:count] == 0, 0.0, pltpu.roll(values, 1, 0))
        after = jnp.where(col[:count] == width - 1, 0.0, pltpu.roll(values, count - 1, 0))
        for c, shifted in enumerate((before, values, after)):
            first = c * both + lane
            wide[window(k, 1), first : first + hidden] = shifted.astype(bf16)

    def conv(weight, k):
        rows = [wide[window(k, r), :] for r in range(3)]
        return dot(jnp.concatenate(rows, axis=1), weight[...].reshape(taps * both, -1))

    field[pl.ds(here, local), :] = context[...].astype(f32)
    field[pl.ds(there, beyond), :] = halo[:, hidden:].astype(f32)
    spread(field[...], hidden, 0)
    field[pl.ds(here, local), :] = state[...].astype(f32)
    field[pl.ds(there, beyond), :] = halo[:, :hidden].astype(f32)
    spread(field[...], 0, 0)
    for k in range(1, 2 * ITERS, 2):
        gates = conv(w_gates, k)
        fresh[window(k), :] = jax.nn.sigmoid(gates[:, :hidden])
        reset = jax.nn.sigmoid(gates[:, hidden:])
        spread((reset * field[window(k), :]).astype(bf16).astype(f32), 0, k)
        cand = jnp.tanh(conv(w_cand, k + 1))
        update = fresh[window(k + 1), :]
        now = (1.0 - update) * field[window(k + 1), :] + update * cand
        if k + 1 < 2 * ITERS:
            now = now.astype(bf16).astype(f32)
            field[window(k + 1), :] = now
            spread(now, 0, k + 1)
    out[...] = now.astype(bf16)


def output_body(returned, tokens, w_out, out):
    rows = returned.shape[0] // 2
    for i in range(2):
        mine = slice(turned(i, 2) * rows, (turned(i, 2) + 1) * rows)
        added = dot(returned[i * rows : (i + 1) * rows, :], w_out[...])
        out[mine, :] = (tokens[mine, :].astype(f32) + added).astype(bf16)


def on_device(
    pixels,
    gru_state,
    tokens,
    visible,
    query_frame,
    pixel_query,
    pixel_key,
    pixel_value,
    pixel_out,
    time_query,
    time_key,
    time_value,
    time_out,
    gru_gates,
    gru_candidate,
):
    frames = lax.axis_size("frame")
    _, band_rows, width, channels = pixels.shape
    hidden = gru_state.shape[3]
    half = tokens.shape[1]
    share = half // frames
    local = band_rows * width
    beyond = 2 * ITERS * width
    assert LANES % share == 0
    assert lax.axis_size("band") == 2 and channels == 2 * LANES and hidden == LANES
    swap = [(0, 1), (1, 0)]
    local_tokens = tokens[0]
    flat_state = gru_state.reshape(local, hidden)
    groups = half // LANES

    other = lax.ppermute(local_tokens, "band", swap)
    flags = lax.ppermute(visible, "band", swap)
    packed = call(
        pack_body,
        jax.ShapeDtypeStruct((frames, 2 * share + MASK_ROWS, LANES), bf16),
        (),
        scratch=[
            pltpu.VMEM((groups, LANES), jnp.int32),
            pltpu.VMEM((frames, 2 * share + MASK_ROWS, LANES), bf16),
            pltpu.SemaphoreType.DMA((13,)),
        ],
        raw=(local_tokens.reshape(frames, share, channels), visible.reshape(groups, LANES)),
        flops=10**10,
        grant=60 * 2**20,
        place=HBM,
    )
    arrived = exchange(packed)

    query, key, value, w_time, w_out = call(
        project_body,
        (
            jax.ShapeDtypeStruct((local, channels), bf16),
            jax.ShapeDtypeStruct((half, channels), bf16),
            jax.ShapeDtypeStruct((half, channels), bf16),
            jax.ShapeDtypeStruct((3 * channels, channels), bf16),
            jax.ShapeDtypeStruct((channels, channels), bf16),
        ),
        (
            pixels.reshape(local, channels),
            local_tokens,
            pixel_query,
            pixel_key,
            pixel_value,
            time_query,
            time_key,
            time_value,
            time_out,
        ),
        flops=2 * (local + 2 * half) * channels * channels,
    )
    context, edge = call(
        attend_body,
        (
            jax.ShapeDtypeStruct((local, hidden), bf16),
            jax.ShapeDtypeStruct((beyond, 2 * hidden), bf16),
        ),
        (query, key, value, other, visible, flags, pixel_key, pixel_value, pixel_out, flat_state),
        flops=4 * local * 2 * half * channels * HEADS,
    )
    halo = lax.ppermute(edge, "band", swap)

    attended = call(
        temporal_body,
        jax.ShapeDtypeStruct((frames, share, channels), bf16),
        (arrived, query_frame.reshape(groups, LANES), w_time),
        after=(edge,),
        scratch=[
            pltpu.VMEM((frames, share, channels), bf16),
            pltpu.SemaphoreType.DMA((frames,)),
        ],
        place=HBM,
        flops=6 * half * channels * channels * 4,
    )
    returned = exchange(attended)

    refined = call(
        refine_body,
        jax.ShapeDtypeStruct((local, hidden), bf16),
        (
            flat_state,
            context,
            halo,
            gru_gates.reshape(9, 2 * hidden, 2 * hidden),
            gru_candidate.reshape(9, 2 * hidden, hidden),
        ),
        scratch=[
            pltpu.VMEM((local + beyond, hidden), f32),
            pltpu.VMEM((local + beyond, hidden), f32),
            pltpu.VMEM((local + beyond + 2 * width, 6 * hidden), bf16),
        ],
        flops=2 * (local + beyond) * 9 * 2 * hidden * 3 * hidden * ITERS,
    )
    track_out = call(
        output_body,
        jax.ShapeDtypeStruct((half, channels), bf16),
        (returned.reshape(half, channels), local_tokens, w_out),
        flops=2 * half * channels * channels,
    )
    return refined.reshape(gru_state.shape), track_out[None]


def solution(mesh):
    placed = (
        P(("clip", "frame"), "band", None, None),
        P(("clip", "frame"), "band", None, None),
        P(("clip", "frame"), "band", None),
        P(("clip", "frame"), "band"),
        P(("clip", "band")),
        P(),
        P(),
        P(),
        P(),
        P(),
        P(),
        P(),
        P(),
        P(),
        P(),
    )
    return jax.shard_map(
        on_device,
        mesh=mesh,
        in_specs=placed,
        out_specs=(P(("clip", "frame"), "band", None, None), P(("clip", "frame"), "band", None)),
        check_vma=False,
    )
```

```python
import jax
import jax.numpy as jnp
from jax import lax
from jax.experimental import pallas as pl
from jax.experimental.pallas import tpu as pltpu
from jax.sharding import PartitionSpec as P

HEADS = 8
ITERS = 2
LANES = 128
MASK_ROWS = 8
HIDDEN = -1e30
LOG2E = 1.4426950408889634

f32 = jnp.float32
bf16 = jnp.bfloat16
VMEM = pl.BlockSpec(memory_space=pltpu.VMEM)
HBM = pl.BlockSpec(memory_space=pltpu.HBM)
LATER = pl.BlockSpec(memory_space=pl.ANY)


def dot(a, b):
    return jnp.dot(a, b, preferred_element_type=f32)


def call(body, out, near, scratch=(), flops=0, after=(), raw=(), grant=24 * 2**20, place=VMEM):
    args = (*raw, *near)
    return pl.pallas_call(
        lambda *refs: body(*refs[len(after) :]),
        out_shape=out,
        in_specs=[LATER] * len(after) + [HBM] * len(raw) + [VMEM] * len(near),
        out_specs=jax.tree.map(lambda _: place, out),
        scratch_shapes=scratch,
        compiler_params=pltpu.CompilerParams(vmem_limit_bytes=grant),
        cost_estimate=pl.CostEstimate(
            flops=flops,
            bytes_accessed=sum(x.size * x.dtype.itemsize for x in args),
            transcendentals=0,
        ),
    )(*after, *args)


def turned(slot, frames):
    return (slot + frames // 2) % frames


def exchange(x):
    frames = lax.axis_size("frame")
    return lax.all_to_all(
        x,
        "frame",
        split_axis=0,
        concat_axis=0,
        tiled=True,
        axis_index_groups=[[turned(i, frames) for i in range(frames)]],
    )


def pack_body(tokens, visible, out, flags, packed, sems):
    frames, rows, _ = out.shape
    share = tokens.shape[1]
    chunks = 4
    step = frames // chunks
    first = pltpu.make_async_copy(visible, flags, sems.at[0])
    first.start()
    coming = []
    for i in range(chunks):
        some = pl.ds(i * step, step)
        coming.append(
            [
                pltpu.make_async_copy(
                    tokens.at[some, :, pl.ds(c * LANES, LANES)],
                    packed.at[some, pl.ds(c * share, share), :],
                    sems.at[1 + 2 * i + c],
                )
                for c in range(2)
            ]
        )
    for copies in coming:
        for copy in copies:
            copy.start()
    first.wait()
    for g in range(frames):
        group = flags[g * share // LANES, :].astype(f32)
        packed[g, 2 * share :, :] = jnp.broadcast_to(group[None], (MASK_ROWS, LANES)).astype(bf16)
    going = []
    for i, copies in enumerate(coming):
        for copy in copies:
            copy.wait()
        some = pl.ds(i * step, step)
        going.append(pltpu.make_async_copy(packed.at[some], out.at[some], sems.at[1 + 2 * chunks + i]))
        going[-1].start()
    for copy in going:
        copy.wait()


def project_body(
    pixels,
    tokens,
    w_query,
    w_key,
    w_value,
    w_time_query,
    w_time_key,
    w_time_value,
    w_time_out,
    query,
    key,
    value,
    w_time,
    w_out,
):
    query[...] = dot(pixels[...], w_query[...]).astype(bf16)
    key[...] = dot(tokens[...], w_key[...]).astype(bf16)
    value[...] = dot(tokens[...], w_value[...]).astype(bf16)
    channels = w_time_out.shape[0]
    line = lax.broadcasted_iota(jnp.int32, (channels, channels), 0)
    column = lax.broadcasted_iota(jnp.int32, (channels, channels), 1)
    order = line % HEADS * (channels // HEADS) + line // HEADS
    order = jnp.where(column == order, 1.0, 0.0).astype(bf16)
    for i, weight in enumerate((w_time_query, w_time_key, w_time_value)):
        moved = lax.dot_general(
            order, weight[...], (((1,), (1,)), ((), ())), preferred_element_type=f32
        )
        w_time[i * channels : (i + 1) * channels, :] = moved.astype(bf16)
    w_out[...] = dot(order, w_time_out[...]).astype(bf16)


def attend_body(
    query, key, value, other, visible, flags, w_key, w_value, w_out, state, context, edge
):
    channels = query.shape[1]
    head_dim = channels // HEADS
    keys = jnp.concatenate([key[...], dot(other[...], w_key[...]).astype(bf16)], axis=0)
    values = jnp.concatenate([value[...], dot(other[...], w_value[...]).astype(bf16)], axis=0)
    tracks = keys.shape[0]
    seen = jnp.concatenate([visible[...], flags[...]], axis=1).astype(f32)
    seen = [seen[:, i * LANES : (i + 1) * LANES] for i in range(tracks // LANES)]
    seen = jnp.concatenate(seen, axis=0).T
    seen = jnp.concatenate([seen[:, i : i + 1] for i in range(tracks // LANES)], axis=0)
    bias = jnp.where(seen > 0.5, 0.0, HIDDEN).astype(bf16)
    lane = lax.broadcasted_iota(jnp.int32, (1, LANES), 1)
    one = jnp.ones((1, 1), bf16)
    scale = LOG2E * head_dim**-0.5
    attended = []
    for tile in range(channels // LANES):
        some = slice(tile * LANES, (tile + 1) * LANES)
        spares = (0, LANES - 1)
        key_of = {x: jnp.where(lane == x, bias, keys[:, some]) for x in spares}
        value_of = {x: jnp.where(lane == x, one, values[:, some]) for x in spares}
        result = jnp.zeros((query.shape[0], LANES), f32)
        for head in range(LANES // head_dim):
            mine = lane // head_dim == head
            spare = spares[0] if head else spares[1]
            asking = jnp.where(mine, query[:, some], jnp.where(lane == spare, one, 0 * one))
            scores = lax.dot_general(
                asking, key_of[spare], (((1,), (1,)), ((), ())), preferred_element_type=f32
            )
            top = jnp.max(scores, axis=1, keepdims=True)
            weights = jnp.exp2((scores - top) * scale).astype(bf16)
            summed = dot(weights, value_of[spare])
            total = summed[:, spare : spare + 1]
            result = jnp.where(mine, summed * (1.0 / total), result)
        attended.append(result.astype(bf16))
    context[...] = dot(jnp.concatenate(attended, axis=1), w_out[...]).astype(bf16)
    count = edge.shape[0]
    start = pl.multiple_of((1 - lax.axis_index("band")) * (query.shape[0] - count), count)
    edge[:, :LANES] = state[pl.ds(start, count), :]
    edge[:, LANES:] = context[pl.ds(start, count), :]


def temporal_body(packed, query_frame, w_all, w_out, out, result, sems):
    frames, share, channels = out.shape
    head_dim = channels // HEADS
    tiles = frames * share // LANES
    beside = LANES // share
    mine = (lax.axis_index("frame") + frames - turned(0, frames)) % frames
    piece = lax.broadcasted_iota(jnp.int32, (1, LANES), 1) // share

    def fold(x, add=jnp.add):
        shift = share
        while shift < LANES:
            x = add(x, pltpu.roll(x, shift, 1))
            shift *= 2
        return x

    def everywhere(x, which):
        return fold(jnp.where(piece == which, x, 0.0))

    def apart(x):
        if beside == 2:
            other = pltpu.roll(x, share, 1)
            return [jnp.where(piece == 0, x, other), jnp.where(piece == 0, other, x)]
        return [everywhere(x, o) for o in range(beside)]

    def together(parts):
        if beside == 2:
            a, b = parts
            other = pltpu.roll(jnp.where(piece == 0, b, a), share, 1)
            return jnp.where(piece == 0, a, b) + other
        x = jnp.zeros_like(parts[0])
        for o, part in enumerate(parts):
            x = jnp.where(piece == o, fold(part), x)
        return x

    asked = query_frame[pl.ds(mine * share // LANES, 1), :].astype(f32)
    asked = everywhere(asked, mine % beside)
    flags = everywhere(packed[:, 2 * share, :].astype(f32), mine % beside)
    seen = []
    for tile in range(tiles):
        row = jnp.zeros((1, LANES), f32)
        for o in range(beside):
            g = tile * beside + o
            row = jnp.where(piece == o, flags[g : g + 1, :], row)
        seen.append(row > 0.5)

    left = packed[:, :share, :].reshape(frames * share, LANES)
    right = packed[:, share : 2 * share, :].reshape(frames * share, LANES)
    rows = jnp.concatenate([left, right], axis=1)
    projected = lax.dot_general(
        w_all[...], rows, (((1,), (1,)), ((), ())), preferred_element_type=f32
    )
    projected = projected.astype(bf16).astype(f32)
    query, key, value = (
        [
            projected[i * channels : (i + 1) * channels, t * LANES : (t + 1) * LANES]
            for t in range(tiles)
        ]
        for i in range(3)
    )
    anchor = jnp.zeros((channels, LANES), f32)
    for tile in range(tiles):
        frame = turned(piece + tile * beside, frames).astype(f32)
        anchor = anchor + jnp.where(asked == frame, query[tile], 0.0)
    anchor = fold(anchor)

    copies = []
    by_head = (head_dim, HEADS, LANES)
    for tile in range(tiles):
        parts = []
        for asking in apart(query[tile]):
            joint = (asking + anchor).astype(bf16).astype(f32)
            scores = []
            for other in range(tiles):
                product = (key[other] * joint).reshape(by_head)
                score = jnp.sum(product, axis=0) * head_dim**-0.5
                scores.append(jnp.where(seen[other], score, HIDDEN))
            top = scores[0]
            for score in scores[1:]:
                top = jnp.maximum(top, score)
            top = fold(top, jnp.maximum)
            raised = [jnp.exp(score - top) for score in scores]
            total = fold(sum(raised[1:], raised[0]))
            summed = None
            for other in range(tiles):
                weight = (raised[other] / total).astype(bf16).astype(f32)
                term = value[other].reshape(by_head) * weight[None]
                summed = term if summed is None else summed + term
            parts.append(summed.reshape(channels, LANES))
        some = pl.ds(tile * beside, beside)
        added = dot(together(parts).T.astype(bf16), w_out[...])
        total = rows[tile * LANES : (tile + 1) * LANES, :].astype(f32) + added
        result[some] = total.astype(bf16).reshape(beside, share, channels)
        copies.append(pltpu.make_async_copy(result.at[some], out.at[some], sems.at[tile]))
        copies[-1].start()
    for copy in copies:
        copy.wait()


def refine_body(state, context, halo, w_gates, w_cand, out, field, fresh, wide):
    taps, both, _ = w_gates.shape
    local, hidden = state.shape
    beyond = halo.shape[0]
    pixels = local + beyond
    width = (wide.shape[0] - pixels) // 2
    band = lax.axis_index("band")
    here = pl.multiple_of(band * beyond, beyond)
    there = pl.multiple_of((1 - band) * local, beyond)
    col = lax.broadcasted_iota(jnp.int32, (pixels, hidden), 0) % width
    wide[:width, :] = jnp.zeros((width, 3 * both), bf16)
    wide[width + pixels :, :] = jnp.zeros((width, 3 * both), bf16)

    def window(k, below=0):
        start = pl.multiple_of(band * k * width, width) + below * width
        return pl.ds(pl.multiple_of(start, width), pixels - k * width)

    def spread(values, lane, k):
        count = values.shape[0]
        before = jnp.where(col[:count] == 0, 0.0, pltpu.roll(values, 1, 0))
        after = jnp.where(col[:count] == width - 1, 0.0, pltpu.roll(values, count - 1, 0))
        for c, shifted in enumerate((before, values, after)):
            first = c * both + lane
            wide[window(k, 1), first : first + hidden] = shifted.astype(bf16)

    def conv(weight, k):
        rows = [wide[window(k, r), :] for r in range(3)]
        return dot(jnp.concatenate(rows, axis=1), weight[...].reshape(taps * both, -1))

    field[pl.ds(here, local), :] = context[...].astype(f32)
    field[pl.ds(there, beyond), :] = halo[:, hidden:].astype(f32)
    spread(field[...], hidden, 0)
    field[pl.ds(here, local), :] = state[...].astype(f32)
    field[pl.ds(there, beyond), :] = halo[:, :hidden].astype(f32)
    spread(field[...], 0, 0)
    for k in range(1, 2 * ITERS, 2):
        gates = conv(w_gates, k)
        fresh[window(k), :] = jax.nn.sigmoid(gates[:, :hidden])
        reset = jax.nn.sigmoid(gates[:, hidden:])
        spread((reset * field[window(k), :]).astype(bf16).astype(f32), 0, k)
        cand = jnp.tanh(conv(w_cand, k + 1))
        update = fresh[window(k + 1), :]
        now = (1.0 - update) * field[window(k + 1), :] + update * cand
        if k + 1 < 2 * ITERS:
            now = now.astype(bf16).astype(f32)
            field[window(k + 1), :] = now
            spread(now, 0, k + 1)
    out[...] = now.astype(bf16)


def on_device(
    pixels,
    gru_state,
    tokens,
    visible,
    query_frame,
    pixel_query,
    pixel_key,
    pixel_value,
    pixel_out,
    time_query,
    time_key,
    time_value,
    time_out,
    gru_gates,
    gru_candidate,
):
    frames = lax.axis_size("frame")
    _, band_rows, width, channels = pixels.shape
    hidden = gru_state.shape[3]
    half = tokens.shape[1]
    share = half // frames
    local = band_rows * width
    beyond = 2 * ITERS * width
    assert LANES % share == 0
    assert lax.axis_size("band") == 2 and channels == 2 * LANES and hidden == LANES
    swap = [(0, 1), (1, 0)]
    local_tokens = tokens[0]
    flat_state = gru_state.reshape(local, hidden)
    groups = half // LANES

    other = lax.ppermute(local_tokens, "band", swap)
    flags = lax.ppermute(visible, "band", swap)
    packed = call(
        pack_body,
        jax.ShapeDtypeStruct((frames, 2 * share + MASK_ROWS, LANES), bf16),
        (),
        scratch=[
            pltpu.VMEM((groups, LANES), jnp.int32),
            pltpu.VMEM((frames, 2 * share + MASK_ROWS, LANES), bf16),
            pltpu.SemaphoreType.DMA((13,)),
        ],
        raw=(local_tokens.reshape(frames, share, channels), visible.reshape(groups, LANES)),
        flops=10**10,
        grant=60 * 2**20,
        place=HBM,
    )
    arrived = exchange(packed)

    query, key, value, w_time, w_out = call(
        project_body,
        (
            jax.ShapeDtypeStruct((local, channels), bf16),
            jax.ShapeDtypeStruct((half, channels), bf16),
            jax.ShapeDtypeStruct((half, channels), bf16),
            jax.ShapeDtypeStruct((3 * channels, channels), bf16),
            jax.ShapeDtypeStruct((channels, channels), bf16),
        ),
        (
            pixels.reshape(local, channels),
            local_tokens,
            pixel_query,
            pixel_key,
            pixel_value,
            time_query,
            time_key,
            time_value,
            time_out,
        ),
        flops=2 * (local + 2 * half) * channels * channels,
    )
    context, edge = call(
        attend_body,
        (
            jax.ShapeDtypeStruct((local, hidden), bf16),
            jax.ShapeDtypeStruct((beyond, 2 * hidden), bf16),
        ),
        (query, key, value, other, visible, flags, pixel_key, pixel_value, pixel_out, flat_state),
        flops=4 * local * 2 * half * channels * HEADS,
    )
    halo = lax.ppermute(edge, "band", swap)

    tracked = call(
        temporal_body,
        jax.ShapeDtypeStruct((frames, share, channels), bf16),
        (arrived, query_frame.reshape(groups, LANES), w_time, w_out),
        after=(edge,),
        scratch=[
            pltpu.VMEM((frames, share, channels), bf16),
            pltpu.SemaphoreType.DMA((frames,)),
        ],
        place=HBM,
        flops=6 * half * channels * channels * 4,
    )
    track_out = exchange(tracked)

    refined = call(
        refine_body,
        jax.ShapeDtypeStruct((local, hidden), bf16),
        (
            flat_state,
            context,
            halo,
            gru_gates.reshape(9, 2 * hidden, 2 * hidden),
            gru_candidate.reshape(9, 2 * hidden, hidden),
        ),
        scratch=[
            pltpu.VMEM((local + beyond, hidden), f32),
            pltpu.VMEM((local + beyond, hidden), f32),
            pltpu.VMEM((local + beyond + 2 * width, 6 * hidden), bf16),
        ],
        flops=2 * (local + beyond) * 9 * 2 * hidden * 3 * hidden * ITERS,
    )
    return refined.reshape(gru_state.shape), track_out.reshape(tokens.shape)


def solution(mesh):
    placed = (
        P(("clip", "frame"), "band", None, None),
        P(("clip", "frame"), "band", None, None),
        P(("clip", "frame"), "band", None),
        P(("clip", "frame"), "band"),
        P(("clip", "band")),
        P(),
        P(),
        P(),
        P(),
        P(),
        P(),
        P(),
        P(),
        P(),
        P(),
    )
    return jax.shard_map(
        on_device,
        mesh=mesh,
        in_specs=placed,
        out_specs=(P(("clip", "frame"), "band", None, None), P(("clip", "frame"), "band", None)),
        check_vma=False,
    )
```

```python
import jax
import jax.numpy as jnp
from jax import lax
from jax.experimental import pallas as pl
from jax.experimental.pallas import tpu as pltpu
from jax.sharding import PartitionSpec as P

HEADS = 8
ITERS = 2
LANES = 128
MASK_ROWS = 8
HIDDEN = -1e30
ORDERS = ((4, 3, 7, 6, 2, 0, 5, 1),)
LOG2E = 1.4426950408889634

f32 = jnp.float32
bf16 = jnp.bfloat16
VMEM = pl.BlockSpec(memory_space=pltpu.VMEM)
HBM = pl.BlockSpec(memory_space=pltpu.HBM)
LATER = pl.BlockSpec(memory_space=pl.ANY)


def dot(a, b):
    return jnp.dot(a, b, preferred_element_type=f32)


def call(body, out, near, scratch=(), flops=0, after=(), raw=(), grant=24 * 2**20, place=VMEM):
    args = (*raw, *near)
    return pl.pallas_call(
        lambda *refs: body(*refs[len(after) :]),
        out_shape=out,
        in_specs=[LATER] * len(after) + [HBM] * len(raw) + [VMEM] * len(near),
        out_specs=jax.tree.map(lambda _: place, out),
        scratch_shapes=scratch,
        compiler_params=pltpu.CompilerParams(vmem_limit_bytes=grant),
        cost_estimate=pl.CostEstimate(
            flops=flops,
            bytes_accessed=sum(x.size * x.dtype.itemsize for x in args),
            transcendentals=0,
        ),
    )(*after, *args)


def group_order(frames):
    for order in ORDERS:
        if len(order) == frames:
            return list(order)
    return [(slot + frames // 2) % frames for slot in range(frames)]


def exchange(x):
    frames = lax.axis_size("frame")
    return lax.all_to_all(
        x,
        "frame",
        split_axis=0,
        concat_axis=0,
        tiled=True,
        axis_index_groups=[group_order(frames)],
    )


def pack_body(tokens, visible, out, flags, packed, sems):
    frames, rows, _ = out.shape
    share = tokens.shape[1]
    chunks = 4
    step = frames // chunks
    first = pltpu.make_async_copy(visible, flags, sems.at[0])
    first.start()
    coming = []
    for i in range(chunks):
        some = pl.ds(i * step, step)
        coming.append(
            [
                pltpu.make_async_copy(
                    tokens.at[some, :, pl.ds(c * LANES, LANES)],
                    packed.at[some, pl.ds(c * share, share), :],
                    sems.at[1 + 2 * i + c],
                )
                for c in range(2)
            ]
        )
    for copies in coming:
        for copy in copies:
            copy.start()
    first.wait()
    for g in range(frames):
        group = flags[g * share // LANES, :].astype(f32)
        packed[g, 2 * share :, :] = jnp.broadcast_to(group[None], (MASK_ROWS, LANES)).astype(bf16)
    going = []
    for i, copies in enumerate(coming):
        for copy in copies:
            copy.wait()
        some = pl.ds(i * step, step)
        going.append(pltpu.make_async_copy(packed.at[some], out.at[some], sems.at[1 + 2 * chunks + i]))
        going[-1].start()
    for copy in going:
        copy.wait()


def project_body(
    pixels,
    tokens,
    w_query,
    w_key,
    w_value,
    w_time_query,
    w_time_key,
    w_time_value,
    w_time_out,
    query,
    key,
    value,
    w_time,
    w_out,
):
    query[...] = dot(pixels[...], w_query[...]).astype(bf16)
    key[...] = dot(tokens[...], w_key[...]).astype(bf16)
    value[...] = dot(tokens[...], w_value[...]).astype(bf16)
    channels = w_time_out.shape[0]
    line = lax.broadcasted_iota(jnp.int32, (channels, channels), 0)
    column = lax.broadcasted_iota(jnp.int32, (channels, channels), 1)
    order = line % HEADS * (channels // HEADS) + line // HEADS
    order = jnp.where(column == order, 1.0, 0.0).astype(bf16)
    for i, weight in enumerate((w_time_query, w_time_key, w_time_value)):
        moved = lax.dot_general(
            order, weight[...], (((1,), (1,)), ((), ())), preferred_element_type=f32
        )
        w_time[i * channels : (i + 1) * channels, :] = moved.astype(bf16)
    w_out[...] = dot(order, w_time_out[...]).astype(bf16)


def attend_body(
    query, key, value, other, visible, flags, w_key, w_value, w_out, state, context, edge
):
    channels = query.shape[1]
    head_dim = channels // HEADS
    keys = jnp.concatenate([key[...], dot(other[...], w_key[...]).astype(bf16)], axis=0)
    values = jnp.concatenate([value[...], dot(other[...], w_value[...]).astype(bf16)], axis=0)
    tracks = keys.shape[0]
    seen = jnp.concatenate([visible[...], flags[...]], axis=1).astype(f32)
    seen = [seen[:, i * LANES : (i + 1) * LANES] for i in range(tracks // LANES)]
    seen = jnp.concatenate(seen, axis=0).T
    seen = jnp.concatenate([seen[:, i : i + 1] for i in range(tracks // LANES)], axis=0)
    bias = jnp.where(seen > 0.5, 0.0, HIDDEN).astype(bf16)
    lane = lax.broadcasted_iota(jnp.int32, (1, LANES), 1)
    one = jnp.ones((1, 1), bf16)
    scale = LOG2E * head_dim**-0.5
    attended = []
    for tile in range(channels // LANES):
        some = slice(tile * LANES, (tile + 1) * LANES)
        spares = (0, LANES - 1)
        key_of = {x: jnp.where(lane == x, bias, keys[:, some]) for x in spares}
        value_of = {x: jnp.where(lane == x, one, values[:, some]) for x in spares}
        result = jnp.zeros((query.shape[0], LANES), f32)
        for head in range(LANES // head_dim):
            mine = lane // head_dim == head
            spare = spares[0] if head else spares[1]
            asking = jnp.where(mine, query[:, some], jnp.where(lane == spare, one, 0 * one))
            scores = lax.dot_general(
                asking, key_of[spare], (((1,), (1,)), ((), ())), preferred_element_type=f32
            )
            top = jnp.max(scores, axis=1, keepdims=True)
            weights = jnp.exp2((scores - top) * scale).astype(bf16)
            summed = dot(weights, value_of[spare])
            total = summed[:, spare : spare + 1]
            result = jnp.where(mine, summed * (1.0 / total), result)
        attended.append(result.astype(bf16))
    context[...] = dot(jnp.concatenate(attended, axis=1), w_out[...]).astype(bf16)
    count = edge.shape[0]
    start = pl.multiple_of((1 - lax.axis_index("band")) * (query.shape[0] - count), count)
    edge[:, :LANES] = state[pl.ds(start, count), :]
    edge[:, LANES:] = context[pl.ds(start, count), :]


def temporal_body(packed, query_frame, w_all, w_out, out, result, sems):
    frames, share, channels = out.shape
    head_dim = channels // HEADS
    tiles = frames * share // LANES
    beside = LANES // share
    order = group_order(frames)
    me = lax.axis_index("frame")
    mine = 0
    for j in range(1, frames):
        mine = jnp.where(me == order[j], j, mine)
    piece = lax.broadcasted_iota(jnp.int32, (1, LANES), 1) // share

    def fold(x, add=jnp.add):
        shift = share
        while shift < LANES:
            x = add(x, pltpu.roll(x, shift, 1))
            shift *= 2
        return x

    def everywhere(x, which):
        return fold(jnp.where(piece == which, x, 0.0))

    def apart(x):
        if beside == 2:
            other = pltpu.roll(x, share, 1)
            return [jnp.where(piece == 0, x, other), jnp.where(piece == 0, other, x)]
        return [everywhere(x, o) for o in range(beside)]

    def together(parts):
        if beside == 2:
            a, b = parts
            other = pltpu.roll(jnp.where(piece == 0, b, a), share, 1)
            return jnp.where(piece == 0, a, b) + other
        x = jnp.zeros_like(parts[0])
        for o, part in enumerate(parts):
            x = jnp.where(piece == o, fold(part), x)
        return x

    asked = query_frame[pl.ds(mine * share // LANES, 1), :].astype(f32)
    asked = everywhere(asked, mine % beside)
    flags = everywhere(packed[:, 2 * share, :].astype(f32), mine % beside)
    seen = []
    for tile in range(tiles):
        row = jnp.zeros((1, LANES), f32)
        for o in range(beside):
            g = tile * beside + o
            row = jnp.where(piece == o, flags[g : g + 1, :], row)
        seen.append(row > 0.5)

    left = packed[:, :share, :].reshape(frames * share, LANES)
    right = packed[:, share : 2 * share, :].reshape(frames * share, LANES)
    rows = jnp.concatenate([left, right], axis=1)
    projected = lax.dot_general(
        w_all[...], rows, (((1,), (1,)), ((), ())), preferred_element_type=f32
    )
    projected = projected.astype(bf16).astype(f32)
    query, key, value = (
        [
            projected[i * channels : (i + 1) * channels, t * LANES : (t + 1) * LANES]
            for t in range(tiles)
        ]
        for i in range(3)
    )
    anchor = jnp.zeros((channels, LANES), f32)
    for tile in range(tiles):
        frame = jnp.zeros((1, LANES), f32)
        for o in range(beside):
            frame = jnp.where(piece == o, float(order[tile * beside + o]), frame)
        anchor = anchor + jnp.where(asked == frame, query[tile], 0.0)
    anchor = fold(anchor)

    copies = []
    by_head = (head_dim, HEADS, LANES)
    for tile in range(tiles):
        parts = []
        for asking in apart(query[tile]):
            joint = (asking + anchor).astype(bf16).astype(f32)
            scores = []
            for other in range(tiles):
                product = (key[other] * joint).reshape(by_head)
                score = jnp.sum(product, axis=0) * head_dim**-0.5
                scores.append(jnp.where(seen[other], score, HIDDEN))
            top = scores[0]
            for score in scores[1:]:
                top = jnp.maximum(top, score)
            top = fold(top, jnp.maximum)
            raised = [jnp.exp(score - top) for score in scores]
            total = fold(sum(raised[1:], raised[0]))
            summed = None
            for other in range(tiles):
                weight = (raised[other] / total).astype(bf16).astype(f32)
                term = value[other].reshape(by_head) * weight[None]
                summed = term if summed is None else summed + term
            parts.append(summed.reshape(channels, LANES))
        some = pl.ds(tile * beside, beside)
        added = dot(together(parts).T.astype(bf16), w_out[...])
        total = rows[tile * LANES : (tile + 1) * LANES, :].astype(f32) + added
        result[some] = total.astype(bf16).reshape(beside, share, channels)
        copies.append(pltpu.make_async_copy(result.at[some], out.at[some], sems.at[tile]))
        copies[-1].start()
    for copy in copies:
        copy.wait()


def refine_body(state, context, halo, w_gates, w_cand, out, field, fresh, wide):
    taps, both, _ = w_gates.shape
    local, hidden = state.shape
    beyond = halo.shape[0]
    pixels = local + beyond
    width = (wide.shape[0] - pixels) // 2
    band = lax.axis_index("band")
    here = pl.multiple_of(band * beyond, beyond)
    there = pl.multiple_of((1 - band) * local, beyond)
    col = lax.broadcasted_iota(jnp.int32, (pixels, hidden), 0) % width
    wide[:width, :] = jnp.zeros((width, 3 * both), bf16)
    wide[width + pixels :, :] = jnp.zeros((width, 3 * both), bf16)

    def window(k, below=0):
        start = pl.multiple_of(band * k * width, width) + below * width
        return pl.ds(pl.multiple_of(start, width), pixels - k * width)

    def spread(values, lane, k):
        count = values.shape[0]
        before = jnp.where(col[:count] == 0, 0.0, pltpu.roll(values, 1, 0))
        after = jnp.where(col[:count] == width - 1, 0.0, pltpu.roll(values, count - 1, 0))
        for c, shifted in enumerate((before, values, after)):
            first = c * both + lane
            wide[window(k, 1), first : first + hidden] = shifted.astype(bf16)

    def conv(weight, k):
        rows = [wide[window(k, r), :] for r in range(3)]
        return dot(jnp.concatenate(rows, axis=1), weight[...].reshape(taps * both, -1))

    field[pl.ds(here, local), :] = context[...].astype(f32)
    field[pl.ds(there, beyond), :] = halo[:, hidden:].astype(f32)
    spread(field[...], hidden, 0)
    field[pl.ds(here, local), :] = state[...].astype(f32)
    field[pl.ds(there, beyond), :] = halo[:, :hidden].astype(f32)
    spread(field[...], 0, 0)
    for k in range(1, 2 * ITERS, 2):
        gates = conv(w_gates, k)
        fresh[window(k), :] = jax.nn.sigmoid(gates[:, :hidden])
        reset = jax.nn.sigmoid(gates[:, hidden:])
        spread((reset * field[window(k), :]).astype(bf16).astype(f32), 0, k)
        cand = jnp.tanh(conv(w_cand, k + 1))
        update = fresh[window(k + 1), :]
        now = (1.0 - update) * field[window(k + 1), :] + update * cand
        if k + 1 < 2 * ITERS:
            now = now.astype(bf16).astype(f32)
            field[window(k + 1), :] = now
            spread(now, 0, k + 1)
    out[...] = now.astype(bf16)


def on_device(
    pixels,
    gru_state,
    tokens,
    visible,
    query_frame,
    pixel_query,
    pixel_key,
    pixel_value,
    pixel_out,
    time_query,
    time_key,
    time_value,
    time_out,
    gru_gates,
    gru_candidate,
):
    frames = lax.axis_size("frame")
    _, band_rows, width, channels = pixels.shape
    hidden = gru_state.shape[3]
    half = tokens.shape[1]
    share = half // frames
    local = band_rows * width
    beyond = 2 * ITERS * width
    assert LANES % share == 0
    assert lax.axis_size("band") == 2 and channels == 2 * LANES and hidden == LANES
    swap = [(0, 1), (1, 0)]
    local_tokens = tokens[0]
    flat_state = gru_state.reshape(local, hidden)
    groups = half // LANES

    other = lax.ppermute(local_tokens, "band", swap)
    flags = lax.ppermute(visible, "band", swap)
    packed = call(
        pack_body,
        jax.ShapeDtypeStruct((frames, 2 * share + MASK_ROWS, LANES), bf16),
        (),
        scratch=[
            pltpu.VMEM((groups, LANES), jnp.int32),
            pltpu.VMEM((frames, 2 * share + MASK_ROWS, LANES), bf16),
            pltpu.SemaphoreType.DMA((13,)),
        ],
        raw=(local_tokens.reshape(frames, share, channels), visible.reshape(groups, LANES)),
        flops=10**10,
        grant=60 * 2**20,
        place=HBM,
    )
    arrived = exchange(packed)

    query, key, value, w_time, w_out = call(
        project_body,
        (
            jax.ShapeDtypeStruct((local, channels), bf16),
            jax.ShapeDtypeStruct((half, channels), bf16),
            jax.ShapeDtypeStruct((half, channels), bf16),
            jax.ShapeDtypeStruct((3 * channels, channels), bf16),
            jax.ShapeDtypeStruct((channels, channels), bf16),
        ),
        (
            pixels.reshape(local, channels),
            local_tokens,
            pixel_query,
            pixel_key,
            pixel_value,
            time_query,
            time_key,
            time_value,
            time_out,
        ),
        flops=2 * (local + 2 * half) * channels * channels,
    )
    context, edge = call(
        attend_body,
        (
            jax.ShapeDtypeStruct((local, hidden), bf16),
            jax.ShapeDtypeStruct((beyond, 2 * hidden), bf16),
        ),
        (query, key, value, other, visible, flags, pixel_key, pixel_value, pixel_out, flat_state),
        flops=4 * local * 2 * half * channels * HEADS,
    )
    halo = lax.ppermute(edge, "band", swap)

    tracked = call(
        temporal_body,
        jax.ShapeDtypeStruct((frames, share, channels), bf16),
        (arrived, query_frame.reshape(groups, LANES), w_time, w_out),
        after=(edge,),
        scratch=[
            pltpu.VMEM((frames, share, channels), bf16),
            pltpu.SemaphoreType.DMA((frames,)),
        ],
        place=HBM,
        flops=6 * half * channels * channels * 4,
    )
    track_out = exchange(tracked)

    refined = call(
        refine_body,
        jax.ShapeDtypeStruct((local, hidden), bf16),
        (
            flat_state,
            context,
            halo,
            gru_gates.reshape(9, 2 * hidden, 2 * hidden),
            gru_candidate.reshape(9, 2 * hidden, hidden),
        ),
        scratch=[
            pltpu.VMEM((local + beyond, hidden), f32),
            pltpu.VMEM((local + beyond, hidden), f32),
            pltpu.VMEM((local + beyond + 2 * width, 6 * hidden), bf16),
        ],
        flops=2 * (local + beyond) * 9 * 2 * hidden * 3 * hidden * ITERS,
    )
    return refined.reshape(gru_state.shape), track_out.reshape(tokens.shape)


def solution(mesh):
    placed = (
        P(("clip", "frame"), "band", None, None),
        P(("clip", "frame"), "band", None, None),
        P(("clip", "frame"), "band", None),
        P(("clip", "frame"), "band"),
        P(("clip", "band")),
        P(),
        P(),
        P(),
        P(),
        P(),
        P(),
        P(),
        P(),
        P(),
        P(),
    )
    return jax.shard_map(
        on_device,
        mesh=mesh,
        in_specs=placed,
        out_specs=(P(("clip", "frame"), "band", None, None), P(("clip", "frame"), "band", None)),
        check_vma=False,
    )
```

```python
import jax
import jax.numpy as jnp
from jax import lax
from jax.experimental import pallas as pl
from jax.experimental.pallas import tpu as pltpu
from jax.sharding import PartitionSpec as P

HEADS = 8
ITERS = 2
LANES = 128
MASK_ROWS = 16
HIDDEN = -1e30
ORDERS = ((4, 3, 7, 6, 2, 0, 5, 1),)
LOG2E = 1.4426950408889634

f32 = jnp.float32
bf16 = jnp.bfloat16
VMEM = pl.BlockSpec(memory_space=pltpu.VMEM)
HBM = pl.BlockSpec(memory_space=pltpu.HBM)
LATER = pl.BlockSpec(memory_space=pl.ANY)


def dot(a, b):
    return jnp.dot(a, b, preferred_element_type=f32)


def call(body, out, near, scratch=(), flops=0, after=(), raw=(), grant=24 * 2**20, place=VMEM):
    args = (*raw, *near)
    return pl.pallas_call(
        lambda *refs: body(*refs[len(after) :]),
        out_shape=out,
        in_specs=[LATER] * len(after) + [HBM] * len(raw) + [VMEM] * len(near),
        out_specs=jax.tree.map(lambda _: place, out),
        scratch_shapes=scratch,
        compiler_params=pltpu.CompilerParams(vmem_limit_bytes=grant),
        cost_estimate=pl.CostEstimate(
            flops=flops,
            bytes_accessed=sum(x.size * x.dtype.itemsize for x in args),
            transcendentals=0,
        ),
    )(*after, *args)


def group_order(frames):
    for order in ORDERS:
        if len(order) == frames:
            return list(order)
    return [(slot + frames // 2) % frames for slot in range(frames)]


def exchange(x):
    frames = lax.axis_size("frame")
    return lax.all_to_all(
        x,
        "frame",
        split_axis=0,
        concat_axis=0,
        tiled=True,
        axis_index_groups=[group_order(frames)],
    )


def pack_body(tokens, visible, out, flags, packed, sems):
    frames, rows, _ = out.shape
    share = tokens.shape[1]
    chunks = 4
    step = frames // chunks
    first = pltpu.make_async_copy(visible, flags, sems.at[0])
    first.start()
    coming = []
    for i in range(chunks):
        some = pl.ds(i * step, step)
        coming.append(
            [
                pltpu.make_async_copy(
                    tokens.at[some, :, pl.ds(c * LANES, LANES)],
                    packed.at[some, pl.ds(c * share, share), :],
                    sems.at[1 + 2 * i + c],
                )
                for c in range(2)
            ]
        )
    for copies in coming:
        for copy in copies:
            copy.start()
    first.wait()
    for g in range(frames):
        group = flags[g * share // LANES, :].astype(f32)
        packed[g, 2 * share :, :] = jnp.broadcast_to(group[None], (MASK_ROWS, LANES)).astype(bf16)
    going = []
    for i, copies in enumerate(coming):
        for copy in copies:
            copy.wait()
        some = pl.ds(i * step, step)
        going.append(pltpu.make_async_copy(packed.at[some], out.at[some], sems.at[1 + 2 * chunks + i]))
        going[-1].start()
    for copy in going:
        copy.wait()


def project_body(
    pixels,
    tokens,
    w_query,
    w_key,
    w_value,
    w_time_query,
    w_time_key,
    w_time_value,
    w_time_out,
    query,
    key,
    value,
    w_time,
    w_out,
):
    query[...] = dot(pixels[...], w_query[...]).astype(bf16)
    key[...] = dot(tokens[...], w_key[...]).astype(bf16)
    value[...] = dot(tokens[...], w_value[...]).astype(bf16)
    channels = w_time_out.shape[0]
    line = lax.broadcasted_iota(jnp.int32, (channels, channels), 0)
    column = lax.broadcasted_iota(jnp.int32, (channels, channels), 1)
    order = line % HEADS * (channels // HEADS) + line // HEADS
    order = jnp.where(column == order, 1.0, 0.0).astype(bf16)
    for i, weight in enumerate((w_time_query, w_time_key, w_time_value)):
        moved = lax.dot_general(
            order, weight[...], (((1,), (1,)), ((), ())), preferred_element_type=f32
        )
        w_time[i * channels : (i + 1) * channels, :] = moved.astype(bf16)
    w_out[...] = dot(order, w_time_out[...]).astype(bf16)


def attend_body(
    query, key, value, other, visible, flags, w_key, w_value, w_out, state, context, edge
):
    channels = query.shape[1]
    head_dim = channels // HEADS
    keys = jnp.concatenate([key[...], dot(other[...], w_key[...]).astype(bf16)], axis=0)
    values = jnp.concatenate([value[...], dot(other[...], w_value[...]).astype(bf16)], axis=0)
    tracks = keys.shape[0]
    seen = jnp.concatenate([visible[...], flags[...]], axis=1).astype(f32)
    seen = [seen[:, i * LANES : (i + 1) * LANES] for i in range(tracks // LANES)]
    seen = jnp.concatenate(seen, axis=0).T
    seen = jnp.concatenate([seen[:, i : i + 1] for i in range(tracks // LANES)], axis=0)
    bias = jnp.where(seen > 0.5, 0.0, HIDDEN).astype(bf16)
    lane = lax.broadcasted_iota(jnp.int32, (1, LANES), 1)
    one = jnp.ones((1, 1), bf16)
    scale = LOG2E * head_dim**-0.5
    attended = []
    for tile in range(channels // LANES):
        some = slice(tile * LANES, (tile + 1) * LANES)
        spares = (0, LANES - 1)
        key_of = {x: jnp.where(lane == x, bias, keys[:, some]) for x in spares}
        value_of = {x: jnp.where(lane == x, one, values[:, some]) for x in spares}
        result = jnp.zeros((query.shape[0], LANES), f32)
        for head in range(LANES // head_dim):
            mine = lane // head_dim == head
            spare = spares[0] if head else spares[1]
            asking = jnp.where(mine, query[:, some], jnp.where(lane == spare, one, 0 * one))
            scores = lax.dot_general(
                asking, key_of[spare], (((1,), (1,)), ((), ())), preferred_element_type=f32
            )
            top = jnp.max(scores, axis=1, keepdims=True)
            weights = jnp.exp2((scores - top) * scale).astype(bf16)
            summed = dot(weights, value_of[spare])
            total = summed[:, spare : spare + 1]
            result = jnp.where(mine, summed * (1.0 / total), result)
        attended.append(result.astype(bf16))
    context[...] = dot(jnp.concatenate(attended, axis=1), w_out[...]).astype(bf16)
    count = edge.shape[0]
    start = pl.multiple_of((1 - lax.axis_index("band")) * (query.shape[0] - count), count)
    edge[:, :LANES] = state[pl.ds(start, count), :]
    edge[:, LANES:] = context[pl.ds(start, count), :]


def temporal_body(packed, query_frame, w_all, w_out, out, result, sems):
    frames, share, channels = out.shape
    head_dim = channels // HEADS
    tiles = frames * share // LANES
    beside = LANES // share
    order = group_order(frames)
    me = lax.axis_index("frame")
    mine = 0
    for j in range(1, frames):
        mine = jnp.where(me == order[j], j, mine)
    piece = lax.broadcasted_iota(jnp.int32, (1, LANES), 1) // share

    def fold(x, add=jnp.add):
        shift = share
        while shift < LANES:
            x = add(x, pltpu.roll(x, shift, 1))
            shift *= 2
        return x

    def everywhere(x, which):
        return fold(jnp.where(piece == which, x, 0.0))

    def apart(x):
        if beside == 2:
            other = pltpu.roll(x, share, 1)
            return [jnp.where(piece == 0, x, other), jnp.where(piece == 0, other, x)]
        return [everywhere(x, o) for o in range(beside)]

    def together(parts):
        if beside == 2:
            a, b = parts
            other = pltpu.roll(jnp.where(piece == 0, b, a), share, 1)
            return jnp.where(piece == 0, a, b) + other
        x = jnp.zeros_like(parts[0])
        for o, part in enumerate(parts):
            x = jnp.where(piece == o, fold(part), x)
        return x

    asked = query_frame[pl.ds(mine * share // LANES, 1), :].astype(f32)
    asked = everywhere(asked, mine % beside)
    flags = everywhere(packed[:, 2 * share, :].astype(f32), mine % beside)
    seen = []
    for tile in range(tiles):
        row = jnp.zeros((1, LANES), f32)
        for o in range(beside):
            g = tile * beside + o
            row = jnp.where(piece == o, flags[g : g + 1, :], row)
        seen.append(row > 0.5)

    left = packed[:, :share, :].reshape(frames * share, LANES)
    right = packed[:, share : 2 * share, :].reshape(frames * share, LANES)
    rows = jnp.concatenate([left, right], axis=1)
    projected = lax.dot_general(
        w_all[...], rows, (((1,), (1,)), ((), ())), preferred_element_type=f32
    )
    projected = projected.astype(bf16).astype(f32)
    query, key, value = (
        [
            projected[i * channels : (i + 1) * channels, t * LANES : (t + 1) * LANES]
            for t in range(tiles)
        ]
        for i in range(3)
    )
    anchor = jnp.zeros((channels, LANES), f32)
    for tile in range(tiles):
        frame = jnp.zeros((1, LANES), f32)
        for o in range(beside):
            frame = jnp.where(piece == o, float(order[tile * beside + o]), frame)
        anchor = anchor + jnp.where(asked == frame, query[tile], 0.0)
    anchor = fold(anchor)

    copies = []
    by_head = (head_dim, HEADS, LANES)
    for tile in range(tiles):
        parts = []
        for asking in apart(query[tile]):
            joint = (asking + anchor).astype(bf16).astype(f32)
            scores = []
            for other in range(tiles):
                product = (key[other] * joint).reshape(by_head)
                score = jnp.sum(product, axis=0) * head_dim**-0.5
                scores.append(jnp.where(seen[other], score, HIDDEN))
            top = scores[0]
            for score in scores[1:]:
                top = jnp.maximum(top, score)
            top = fold(top, jnp.maximum)
            raised = [jnp.exp(score - top) for score in scores]
            total = fold(sum(raised[1:], raised[0]))
            summed = None
            for other in range(tiles):
                weight = (raised[other] / total).astype(bf16).astype(f32)
                term = value[other].reshape(by_head) * weight[None]
                summed = term if summed is None else summed + term
            parts.append(summed.reshape(channels, LANES))
        some = pl.ds(tile * beside, beside)
        added = dot(together(parts).T.astype(bf16), w_out[...])
        total = rows[tile * LANES : (tile + 1) * LANES, :].astype(f32) + added
        result[some] = total.astype(bf16).reshape(beside, share, channels)
        copies.append(pltpu.make_async_copy(result.at[some], out.at[some], sems.at[tile]))
        copies[-1].start()
    for copy in copies:
        copy.wait()


def refine_body(state, context, halo, w_gates, w_cand, out, field, fresh, wide):
    taps, both, _ = w_gates.shape
    local, hidden = state.shape
    beyond = halo.shape[0]
    pixels = local + beyond
    width = (wide.shape[0] - pixels) // 2
    band = lax.axis_index("band")
    here = pl.multiple_of(band * beyond, beyond)
    there = pl.multiple_of((1 - band) * local, beyond)
    col = lax.broadcasted_iota(jnp.int32, (pixels, hidden), 0) % width
    wide[:width, :] = jnp.zeros((width, 3 * both), bf16)
    wide[width + pixels :, :] = jnp.zeros((width, 3 * both), bf16)

    def window(k, below=0):
        start = pl.multiple_of(band * k * width, width) + below * width
        return pl.ds(pl.multiple_of(start, width), pixels - k * width)

    def spread(values, lane, k):
        count = values.shape[0]
        before = jnp.where(col[:count] == 0, 0.0, pltpu.roll(values, 1, 0))
        after = jnp.where(col[:count] == width - 1, 0.0, pltpu.roll(values, count - 1, 0))
        for c, shifted in enumerate((before, values, after)):
            first = c * both + lane
            wide[window(k, 1), first : first + hidden] = shifted.astype(bf16)

    def conv(weight, k):
        rows = [wide[window(k, r), :] for r in range(3)]
        return dot(jnp.concatenate(rows, axis=1), weight[...].reshape(taps * both, -1))

    field[pl.ds(here, local), :] = context[...].astype(f32)
    field[pl.ds(there, beyond), :] = halo[:, hidden:].astype(f32)
    spread(field[...], hidden, 0)
    field[pl.ds(here, local), :] = state[...].astype(f32)
    field[pl.ds(there, beyond), :] = halo[:, :hidden].astype(f32)
    spread(field[...], 0, 0)
    for k in range(1, 2 * ITERS, 2):
        gates = conv(w_gates, k)
        fresh[window(k), :] = jax.nn.sigmoid(gates[:, :hidden])
        reset = jax.nn.sigmoid(gates[:, hidden:])
        spread((reset * field[window(k), :]).astype(bf16).astype(f32), 0, k)
        cand = jnp.tanh(conv(w_cand, k + 1))
        update = fresh[window(k + 1), :]
        now = (1.0 - update) * field[window(k + 1), :] + update * cand
        if k + 1 < 2 * ITERS:
            now = now.astype(bf16).astype(f32)
            field[window(k + 1), :] = now
            spread(now, 0, k + 1)
    out[...] = now.astype(bf16)


def on_device(
    pixels,
    gru_state,
    tokens,
    visible,
    query_frame,
    pixel_query,
    pixel_key,
    pixel_value,
    pixel_out,
    time_query,
    time_key,
    time_value,
    time_out,
    gru_gates,
    gru_candidate,
):
    frames = lax.axis_size("frame")
    _, band_rows, width, channels = pixels.shape
    hidden = gru_state.shape[3]
    half = tokens.shape[1]
    share = half // frames
    local = band_rows * width
    beyond = 2 * ITERS * width
    assert LANES % share == 0
    assert lax.axis_size("band") == 2 and channels == 2 * LANES and hidden == LANES
    swap = [(0, 1), (1, 0)]
    local_tokens = tokens[0]
    flat_state = gru_state.reshape(local, hidden)
    groups = half // LANES

    other = lax.ppermute(local_tokens, "band", swap)
    flags = lax.ppermute(visible, "band", swap)
    packed = call(
        pack_body,
        jax.ShapeDtypeStruct((frames, 2 * share + MASK_ROWS, LANES), bf16),
        (),
        scratch=[
            pltpu.VMEM((groups, LANES), jnp.int32),
            pltpu.VMEM((frames, 2 * share + MASK_ROWS, LANES), bf16),
            pltpu.SemaphoreType.DMA((13,)),
        ],
        raw=(local_tokens.reshape(frames, share, channels), visible.reshape(groups, LANES)),
        flops=10**10,
        grant=60 * 2**20,
        place=HBM,
    )
    arrived = exchange(packed)

    query, key, value, w_time, w_out = call(
        project_body,
        (
            jax.ShapeDtypeStruct((local, channels), bf16),
            jax.ShapeDtypeStruct((half, channels), bf16),
            jax.ShapeDtypeStruct((half, channels), bf16),
            jax.ShapeDtypeStruct((3 * channels, channels), bf16),
            jax.ShapeDtypeStruct((channels, channels), bf16),
        ),
        (
            pixels.reshape(local, channels),
            local_tokens,
            pixel_query,
            pixel_key,
            pixel_value,
            time_query,
            time_key,
            time_value,
            time_out,
        ),
        flops=2 * (local + 2 * half) * channels * channels,
    )
    context, edge = call(
        attend_body,
        (
            jax.ShapeDtypeStruct((local, hidden), bf16),
            jax.ShapeDtypeStruct((beyond, 2 * hidden), bf16),
        ),
        (query, key, value, other, visible, flags, pixel_key, pixel_value, pixel_out, flat_state),
        flops=4 * local * 2 * half * channels * HEADS,
    )
    halo = lax.ppermute(edge, "band", swap)

    tracked = call(
        temporal_body,
        jax.ShapeDtypeStruct((frames, share, channels), bf16),
        (arrived, query_frame.reshape(groups, LANES), w_time, w_out),
        after=(edge,),
        scratch=[
            pltpu.VMEM((frames, share, channels), bf16),
            pltpu.SemaphoreType.DMA((frames,)),
        ],
        place=HBM,
        flops=6 * half * channels * channels * 4,
    )
    track_out = exchange(tracked)

    refined = call(
        refine_body,
        jax.ShapeDtypeStruct((local, hidden), bf16),
        (
            flat_state,
            context,
            halo,
            gru_gates.reshape(9, 2 * hidden, 2 * hidden),
            gru_candidate.reshape(9, 2 * hidden, hidden),
        ),
        scratch=[
            pltpu.VMEM((local + beyond, hidden), f32),
            pltpu.VMEM((local + beyond, hidden), f32),
            pltpu.VMEM((local + beyond + 2 * width, 6 * hidden), bf16),
        ],
        flops=2 * (local + beyond) * 9 * 2 * hidden * 3 * hidden * ITERS,
    )
    return refined.reshape(gru_state.shape), track_out.reshape(tokens.shape)


def solution(mesh):
    placed = (
        P(("clip", "frame"), "band", None, None),
        P(("clip", "frame"), "band", None, None),
        P(("clip", "frame"), "band", None),
        P(("clip", "frame"), "band"),
        P(("clip", "band")),
        P(),
        P(),
        P(),
        P(),
        P(),
        P(),
        P(),
        P(),
        P(),
        P(),
    )
    return jax.shard_map(
        on_device,
        mesh=mesh,
        in_specs=placed,
        out_specs=(P(("clip", "frame"), "band", None, None), P(("clip", "frame"), "band", None)),
        check_vma=False,
    )
```
